32 devices in a mesh: grp: 2 (over x), row: 16 (over z, y, core).
Axes of the slice: x: 2, y: 2, z: 4, core: 2. Of those that a mesh axis runs over, the one named last changes fastest.
Arguments:
- facet_rows: bfloat16 [2, 16, 1024, 128], P(None, None, ('grp', 'row')), parts along dimension 2, may hold values from -6 to 6
- range_start: int32 [64], P('grp'), parts along dimension 0, may hold values from 0 to 511, as said below
- range_length: int32 [64], P('grp'), parts along dimension 0, may hold values from 128 to 256, as said below
- facet_offset: int32 [32], P('grp'), parts along dimension 0, may hold values from 0 to 511
- window_table: float32 [16, 256], replicated, may hold values from 0.25 to 1
- kernel_table: float32 [256, 8], replicated, may hold values from 0.05 to 0.5
- cell_row: int32 [64, 8192], P(('grp', 'row')), parts along dimension 0, may hold values from 0 to 248
- cell_column: int32 [64, 8192], P(('grp', 'row')), parts along dimension 0, may hold values from 0 to 248
- kernel_row: int32 [64, 8192], P(('grp', 'row')), parts along dimension 0, may hold values from 0 to 255
- kernel_column: int32 [64, 8192], P(('grp', 'row')), parts along dimension 0, may hold values from 0 to 255
Outputs:
- visibilities: float32 [2, 64, 8192], P(None, 'grp', 'row'), parts along dimension 1
The draws below stay inside these ranges and needn't reach their ends.
There are 2 independent parts, one for each index of `grp`. The reference program is written for one: setup_inputs(seed, part) draws one part's arguments, and reference() takes and returns one part's arrays. A program takes and returns all parts, laid end to end along the dimension named above; an argument that names none is the same for every part. Nothing has to cross between parts.
Inputs may be any that keep to these rules, and one draw needn't show every extreme that they name: Subgrid s is held by row index e = s // 2; its range, range_start[s] to range_start[s] + range_length[s] - 1 taken modulo 512, lies within u from e * 32 - 256 // 2 to (e + 1) * 32 + 256 // 2 - 1 modulo 512. `range_length`: ranges of uneven length.
All inputs are finite; a program needn't handle non-finite values.
Results may differ from the reference program's by a relative error of at most 0.0057.
Values may be sent and summed in bfloat16 or wider, within the bound.
No kernel may reach another device: no remote copies, remote signals or barrier semaphores. Data moves between devices by JAX's collectives and lax.ppermute only.
A program may use at most 64 MiB of HBM per device.

```python
import math
import jax
import jax.numpy as jnp
from jax import lax

F = 16
KC = 128
SUB = 256
R_DEV = 32
SUB_DEV = 2
VPS = 8192
SUPPORT = 8
NOVER = 256
NU = 512
NSUB = 32


def range_pair(key):
    folded = jax.random.fold_in(key, 11)
    key_length, key_shift, key_first, key_second = jax.random.split(folded, 4)
    subgrid_index = jnp.arange(NSUB, dtype=jnp.int32)
    lengths = jax.random.randint(key_length, (NSUB,), SUB // 2, SUB + 1, dtype=jnp.int32)
    first_pick = jax.random.randint(key_first, (), 0, NSUB, dtype=jnp.int32)
    second_pick = (first_pick + 1 + jax.random.randint(key_second, (), 0, NSUB - 1, dtype=jnp.int32)) % NSUB
    lengths = jnp.where(subgrid_index == first_pick, SUB, lengths)
    lengths = jnp.where(subgrid_index == second_pick, SUB // 2, lengths)
    shifts = jax.random.randint(key_shift, (NSUB,), 0, R_DEV, dtype=jnp.int32)
    owners = subgrid_index // SUB_DEV
    starts = (owners * R_DEV + shifts - SUB // 2 + (SUB - lengths) // 2) % NU
    return (starts.astype(jnp.int32), lengths.astype(jnp.int32))


def draw_range_start(key, part):
    return range_pair(key)[0]


def draw_range_length(key, part):
    return range_pair(key)[1]


def set_ends(values, stream_key, least, largest):
    place = [jax.random.randint(jax.random.fold_in(stream_key, axis), (), 0, length) for axis, length in enumerate(values.shape)]
    longest = values.shape.index(max(values.shape))
    neighbour = place[:longest] + [(place[longest] + 1) % values.shape[longest]] + place[longest + 1:]
    return values.at[tuple(place)].set(least).at[tuple(neighbour)].set(largest)


def block_levels(key, shape, cuts, low, top_value):
    factor_of, own = 1.0, jax.random.fold_in(key, 6)
    for dim, shards_of in cuts:
        draws = jnp.exp(jax.random.uniform(jax.random.fold_in(own, dim), (shards_of,), jnp.float32, low / len(cuts), top_value / len(cuts)))
        factor_of = factor_of * jnp.repeat(draws, shape[dim] // shards_of).reshape([-1 if axis == dim else 1 for axis in range(len(shape))])
    return factor_of


def gaussian(stream_key, extent, scale, bound, shards=(), held_as=jnp.bfloat16):
    result = scale * jax.random.normal(stream_key, extent, jnp.float32)
    if shards:
        result = result * block_levels(stream_key, extent, shards, -0.22, 0.18)
    return jnp.clip(result, -bound, bound).astype(held_as)


def setup_inputs(seed: int = 0, part: int = 0) -> dict:
    seeds = jax.random.split(jax.random.key(seed), 11)
    part_keys = jax.random.split(jax.random.fold_in(seeds[10], part), 11)
    facet_rows = gaussian(part_keys[0], (2, F, NU, KC), 1.0, 6.0, ((2, 16),))
    range_start = draw_range_start(jax.random.fold_in(jax.random.fold_in(seeds[10], part), 71), part)
    range_length = draw_range_length(jax.random.fold_in(jax.random.fold_in(seeds[10], part), 71), part)
    facet_offset = set_ends(jax.random.randint(part_keys[3], (F,), 0, NU), jax.random.fold_in(part_keys[3], 1), 0, NU - 1).astype(jnp.int32)
    window_table = jnp.clip(jnp.exp(jax.random.uniform(seeds[4], (F, SUB), jnp.float32, math.log(0.25), math.log(1.0))), 0.25, 1.0)
    kernel_table = jnp.clip(jax.random.uniform(seeds[5], (NOVER, SUPPORT), jnp.float32, 0.05, 0.5), 0.05, 0.5)
    cell_row = set_ends(jax.random.randint(part_keys[6], (NSUB, VPS), 0, SUB - SUPPORT + 1), jax.random.fold_in(part_keys[6], 1), 0, SUB - SUPPORT).astype(jnp.int32)
    cell_column = set_ends(jax.random.randint(part_keys[7], (NSUB, VPS), 0, SUB - SUPPORT + 1), jax.random.fold_in(part_keys[7], 1), 0, SUB - SUPPORT).astype(jnp.int32)
    kernel_row = set_ends(jax.random.randint(part_keys[8], (NSUB, VPS), 0, NOVER), jax.random.fold_in(part_keys[8], 1), 0, NOVER - 1).astype(jnp.int32)
    kernel_column = set_ends(jax.random.randint(part_keys[9], (NSUB, VPS), 0, NOVER), jax.random.fold_in(part_keys[9], 1), 0, NOVER - 1).astype(jnp.int32)
    return dict(facet_rows=facet_rows, range_start=range_start, range_length=range_length, facet_offset=facet_offset, window_table=window_table, kernel_table=kernel_table, cell_row=cell_row, cell_column=cell_column, kernel_row=kernel_row, kernel_column=kernel_column)


TWO_PI = 2.0 * math.pi

def transform_table():
    kcol = jnp.arange(KC, dtype=jnp.int32)
    jcol = jnp.arange(SUB, dtype=jnp.int32)
    angles = TWO_PI * (kcol[:, None] * jcol[None, :] % SUB).astype(jnp.float32) / SUB
    scale = 1.0 / math.sqrt(KC)
    real_part = (jnp.cos(angles) * scale).astype(jnp.bfloat16)
    imag_part = (jnp.sin(angles) * scale).astype(jnp.bfloat16)
    upper = jnp.concatenate([real_part, imag_part], axis=1)
    lower = jnp.concatenate([-imag_part, real_part], axis=1)
    return jnp.concatenate([upper, lower], axis=0)

def phase_angles(offsets, positions, total_rows):
    return TWO_PI * (offsets[:, None] * positions[None, :] % total_rows).astype(jnp.float32) / total_rows

def facet_sum(gathered, window_rows, phases, inside):
    top_precision = lax.Precision.HIGHEST
    weights = window_rows * inside[None, :]
    cos_w = weights * jnp.cos(phases)
    sin_w = weights * jnp.sin(phases)
    real_out = jnp.einsum('fi,fik->ik', cos_w, gathered[0], precision=top_precision) - jnp.einsum('fi,fik->ik', sin_w, gathered[1], precision=top_precision)
    imag_out = jnp.einsum('fi,fik->ik', cos_w, gathered[1], precision=top_precision) + jnp.einsum('fi,fik->ik', sin_w, gathered[0], precision=top_precision)
    return jnp.concatenate([real_out, imag_out], axis=1)

def reference(facet_rows, range_start, range_length, facet_offset, window_table, kernel_table, cell_row, cell_column, kernel_row, kernel_column):
    top_precision = lax.Precision.HIGHEST
    facet_float = facet_rows.astype(jnp.float32)
    transform = transform_table()
    near_table = lax.optimization_barrier(kernel_table.astype(jnp.bfloat16)).astype(jnp.float32)
    kernel_taps = jnp.arange(SUPPORT, dtype=jnp.int32)
    slot_index = jnp.arange(SUB, dtype=jnp.int32)

    def one_subgrid(subgrid):
        positions = (range_start[subgrid] + slot_index) % NU
        gathered = jnp.take(facet_float, positions, axis=2)
        inside = (slot_index < range_length[subgrid]).astype(jnp.float32)
        phases = phase_angles(facet_offset, positions, NU)
        summed_rows = facet_sum(gathered, window_table, phases, inside).astype(jnp.bfloat16)
        subgrid_cells = jnp.dot(summed_rows, transform, preferred_element_type=jnp.float32).astype(jnp.bfloat16)
        subgrid_cells = lax.optimization_barrier(subgrid_cells).astype(jnp.float32)
        row_cells = cell_row[subgrid][:, None, None] + kernel_taps[None, :, None]
        col_cells = cell_column[subgrid][:, None, None] + kernel_taps[None, None, :]
        real_patch = subgrid_cells[row_cells, col_cells]
        imaginary_patch = subgrid_cells[row_cells, col_cells + SUB]
        row_weight = near_table[kernel_row[subgrid]]
        column_weight = kernel_table[kernel_column[subgrid]]
        real_visibility = jnp.einsum('tm,tc,tmc->t', row_weight, column_weight, real_patch, precision=top_precision)
        imaginary_visibility = jnp.einsum('tm,tc,tmc->t', row_weight, column_weight, imaginary_patch, precision=top_precision)
        return jnp.stack([real_visibility, imaginary_visibility])
    stacked = lax.map(one_subgrid, jnp.arange(NSUB, dtype=jnp.int32))
    return jnp.transpose(stacked, (1, 0, 2))
```

```python
import math

import jax
import jax.numpy as jnp
import numpy as np
from jax import lax
from jax.experimental import pallas as pl
from jax.experimental.pallas import tpu as pltpu
from jax.sharding import PartitionSpec as P

F = 16
KC = 128
SUB = 256
R_DEV = 32
SUB_DEV = 2
SUPPORT = 8
NOVER = 256
CHIP = 2 * R_DEV
LANES = 128

TWO_PI = 2.0 * math.pi

VMEM = pl.BlockSpec(memory_space=pltpu.VMEM)
SMEM = pl.BlockSpec(memory_space=pltpu.SMEM)


def transform_table():
    kcol = np.arange(KC)
    jcol = np.arange(SUB)
    angles = np.float32(TWO_PI) * (kcol[:, None] * jcol[None, :] % SUB).astype(np.float32) / np.float32(SUB)
    scale = np.float32(1.0 / math.sqrt(KC))
    real_part = (np.cos(angles) * scale).astype(jnp.bfloat16)
    imag_part = (np.sin(angles) * scale).astype(jnp.bfloat16)
    upper = np.concatenate([real_part, imag_part], axis=1)
    lower = np.concatenate([-imag_part, real_part], axis=1)
    return np.ascontiguousarray(np.concatenate([upper, lower], axis=0).T)


def partners(chip, chips):
    return [
        chip ^ 1,
        (((chip + 1) ^ 1) + chips - 1) % chips,
        chip ^ 2,
        (((chip + 2) ^ 2) + chips - 2) % chips,
    ]


def facet_kernel(
    devices,
    start_ref,
    length_ref,
    offset_ref,
    window_ref,
    own_ref,
    other_ref,
    *rest,
):
    outs, padded = rest[:5], rest[5]
    total_rows = devices * R_DEV
    chips = devices // 2
    position = lax.axis_index("row")
    chip = position // 2
    core = position % 2
    padded[:R_DEV, :] = jnp.zeros((R_DEV, F), jnp.float32)
    padded[R_DEV + SUB :, :] = jnp.zeros((R_DEV, F), jnp.float32)
    padded[R_DEV : R_DEV + SUB, :] = jnp.transpose(window_ref[...])
    targets = [chip] + partners(chip, chips)
    row_index = lax.broadcasted_iota(jnp.int32, (R_DEV, F), 0)
    for held, source in enumerate((own_ref, other_ref)):
        half = core if held == 0 else 1 - core
        base = chip * CHIP + half * R_DEV
        turns = (offset_ref[...] * (base + row_index)) & (total_rows - 1)
        angles = TWO_PI * turns.astype(jnp.float32) / total_rows
        cosines = jnp.cos(angles)
        sines = jnp.sin(angles)
        weights = []
        for target in targets:
            for sub in range(SUB_DEV):
                subgrid = (target * 2 + core) * SUB_DEV + sub
                slot = (base - start_ref[subgrid]) & (total_rows - 1)
                slot = jnp.where(slot > total_rows - R_DEV, slot - total_rows, slot)
                slot = jnp.minimum(slot, SUB)
                piece = padded[pl.ds(slot + R_DEV, R_DEV), :]
                weights.append(jnp.where(slot + row_index < length_ref[subgrid], piece, 0.0))
        for tile in range(R_DEV // 16):
            rows = slice(16 * tile, 16 * tile + 16)
            sums = [[None, None] for _ in weights]
            for f in range(F):
                real_in = source[0, f, rows, :].astype(jnp.float32)
                imag_in = source[1, f, rows, :].astype(jnp.float32)
                cos_f = cosines[rows, f : f + 1]
                sin_f = sines[rows, f : f + 1]
                real_part = cos_f * real_in - sin_f * imag_in
                imag_part = cos_f * imag_in + sin_f * real_in
                for entry, weight in zip(sums, weights):
                    w = jnp.broadcast_to(weight[rows, f : f + 1], (16, KC))
                    entry[0] = w * real_part if f == 0 else entry[0] + w * real_part
                    entry[1] = w * imag_part if f == 0 else entry[1] + w * imag_part
            for place, entry in enumerate(sums):
                first = pl.multiple_of((place % SUB_DEV) * CHIP + half * R_DEV + 16 * tile, 16)
                out = outs[place // SUB_DEV]
                out[pl.ds(first, 16), :KC] = entry[0].astype(jnp.bfloat16)
                out[pl.ds(first, 16), KC:] = entry[1].astype(jnp.bfloat16)


def taps(low, high, cell, table_row):
    count = cell.shape[1]
    cell = jnp.broadcast_to(cell, (SUPPORT, count))
    table_row = jnp.broadcast_to(table_row, (SUPPORT, count))
    place = table_row & (LANES - 1)
    picked = []
    for first in range(0, count, LANES):
        index = place[:, first : first + LANES]
        from_low = jnp.take_along_axis(low, index, axis=1, mode="promise_in_bounds")
        from_high = jnp.take_along_axis(high, index, axis=1, mode="promise_in_bounds")
        picked.append(jnp.where(table_row[:, first : first + LANES] < LANES, from_low, from_high))
    weights = jnp.concatenate(picked, axis=1)
    for bit in range(3):
        turned = pltpu.roll(weights, 1 << bit, axis=0)
        weights = jnp.where((cell & (1 << bit)) != 0, turned, weights)
    sublane = lax.broadcasted_iota(jnp.int32, (SUPPORT, count), 0)
    tile = (cell >> 3) + jnp.where(sublane < (cell & 7), 1, 0)
    return weights, tile


def degrid_kernel(
    devices,
    per_dest,
    start_ref,
    table_ref,
    transform_ref,
    own_ref,
    first_ref,
    second_ref,
    third_ref,
    fourth_ref,
    row_ref,
    column_ref,
    row_kernel_ref,
    column_kernel_ref,
    out_ref,
    cells,
    gathered,
):
    position = lax.axis_index("row")
    chip = position // 2
    even = chip % 2 == 0
    table = jnp.transpose(table_ref[...])
    near = table.astype(jnp.bfloat16).astype(jnp.float32)
    near_low, near_high = near[:, :LANES], near[:, LANES:]
    table_low, table_high = table[:, :LANES], table[:, LANES:]
    for sub in range(SUB_DEV):
        rows = slice(sub * CHIP, sub * CHIP + CHIP)
        first, second = first_ref[rows, :], second_ref[rows, :]
        summed = jnp.concatenate(
            [
                own_ref[rows, :],
                jnp.where(even, first, second),
                third_ref[rows, :] + fourth_ref[rows, :],
                jnp.where(even, second, first),
            ],
            axis=0,
        )
        cells[sub] = lax.dot_general(
            transform_ref[...], summed, (((1,), (1,)), ((), ())), preferred_element_type=jnp.float32
        ).astype(jnp.bfloat16)

    def one_dest(dest, carry):
        lanes = pl.ds(pl.multiple_of(dest * per_dest, per_dest), per_dest)
        for sub in range(SUB_DEV):
            subgrid = position * SUB_DEV + sub
            shift = start_ref[subgrid] - chip * CHIP
            cell_row = (row_ref[sub : sub + 1, lanes] + shift) & (SUB - 1)
            weights, tile = taps(near_low, near_high, cell_row, row_kernel_ref[sub : sub + 1, lanes])
            tile = tile & (SUB // 8 - 1)
            odd = (tile & 1) != 0
            pair = (tile >> 1).astype(jnp.float32)
            pairs = jnp.concatenate(
                [jnp.where(odd, -1.0, pair), jnp.where(odd, pair, -1.0)], axis=0
            ).astype(jnp.bfloat16)
            both = jnp.concatenate([weights, weights], axis=0).astype(jnp.bfloat16)
            zero = jnp.zeros_like(both)
            spread = jnp.concatenate(
                [jnp.where(pairs == jnp.bfloat16(t), both, zero) for t in range(SUB // 16)], axis=0
            )
            along = jnp.dot(cells[sub], spread, preferred_element_type=jnp.float32)
            weights, tile = taps(
                table_low, table_high, column_ref[sub : sub + 1, lanes], column_kernel_ref[sub : sub + 1, lanes]
            )
            real_part = along[:8]
            imag_part = along[SUB : SUB + 8]
            for t in range(1, SUB // 8):
                here = tile == t
                real_part = jnp.where(here, along[8 * t : 8 * t + 8], real_part)
                imag_part = jnp.where(here, along[SUB + 8 * t : SUB + 8 * t + 8], imag_part)
            sums = [
                jnp.sum(weights * real_part, axis=0, keepdims=True),
                jnp.sum(weights * imag_part, axis=0, keepdims=True),
            ]
            chunks = per_dest // LANES
            for part in range(2):
                for chunk in range(chunks):
                    gathered[pl.ds(dest * 4 * chunks + (sub * 2 + part) * chunks + chunk, 1), :] = sums[part][
                        :, chunk * LANES : (chunk + 1) * LANES
                    ]
        return carry

    lax.fori_loop(0, devices, one_dest, 0)
    out_ref[...] = gathered[...].astype(jnp.bfloat16)


def place_kernel(devices, chunks, in_ref, out_ref, wide):
    wide[...] = in_ref[...].astype(jnp.float32)
    for part in range(2):
        for chunk in range(chunks):
            out_ref[part, :, chunk * LANES : (chunk + 1) * LANES] = wide[
                pl.ds(part * chunks + chunk, devices * SUB_DEV, stride=2 * chunks), :
            ]


def local(
    facet_rows,
    range_start,
    range_length,
    facet_offset,
    window_table,
    kernel_table,
    cell_row,
    cell_column,
    kernel_row,
    kernel_column,
):
    devices = lax.axis_size("row")
    chips = devices // 2
    slots = cell_row.shape[1]
    per_dest = slots // devices
    chunks = per_dest // LANES
    other_rows = lax.ppermute(facet_rows, "row", [(i, i ^ 1) for i in range(devices)])
    piece = jax.ShapeDtypeStruct((SUB_DEV * CHIP, 2 * KC), jnp.bfloat16)
    pieces = pl.pallas_call(
        lambda *refs: facet_kernel(devices, *refs),
        out_shape=[piece] * 5,
        in_specs=[SMEM, SMEM, VMEM, VMEM, VMEM, VMEM],
        out_specs=[VMEM] * 5,
        scratch_shapes=[pltpu.VMEM((SUB + 2 * R_DEV, F), jnp.float32)],
        name="facet_sums",
    )(range_start, range_length, facet_offset.reshape(1, F), window_table, facet_rows, other_rows)
    came = []
    for pairing in range(4):
        pairs = [
            (2 * chip + core, 2 * partners(chip, chips)[pairing] + core)
            for chip in range(chips)
            for core in range(2)
        ]
        came.append(lax.ppermute(pieces[1 + pairing], "row", pairs))
    rows_out = devices * 4 * chunks
    results = pl.pallas_call(
        lambda *refs: degrid_kernel(devices, per_dest, *refs),
        out_shape=jax.ShapeDtypeStruct((rows_out, LANES), jnp.bfloat16),
        in_specs=[SMEM] + [VMEM] * 11,
        out_specs=VMEM,
        scratch_shapes=[
            pltpu.VMEM((SUB_DEV, 2 * SUB, SUB), jnp.bfloat16),
            pltpu.VMEM((rows_out, LANES), jnp.float32),
        ],
        compiler_params=pltpu.CompilerParams(vmem_limit_bytes=32 * 1024 * 1024),
        name="degrid",
    )(
        range_start,
        kernel_table,
        jnp.asarray(transform_table()),
        pieces[0],
        *came,
        cell_row,
        cell_column,
        kernel_row,
        kernel_column,
    )
    received = lax.all_to_all(
        results.reshape(devices, 4 * chunks, LANES), "row", split_axis=0, concat_axis=0, tiled=True
    )
    return pl.pallas_call(
        lambda *refs: place_kernel(devices, chunks, *refs),
        out_shape=jax.ShapeDtypeStruct((2, devices * SUB_DEV, per_dest), jnp.float32),
        in_specs=[VMEM],
        out_specs=VMEM,
        scratch_shapes=[pltpu.VMEM((rows_out, LANES), jnp.float32)],
        name="place",
    )(received.reshape(rows_out, LANES))


def solution(mesh):
    placed = (
        P(None, None, ("grp", "row"), None),
        P("grp"),
        P("grp"),
        P("grp"),
        P(),
        P(),
        P(("grp", "row"), None),
        P(("grp", "row"), None),
        P(("grp", "row"), None),
        P(("grp", "row"), None),
    )
    return jax.shard_map(
        local, mesh=mesh, in_specs=placed, out_specs=P(None, "grp", "row"), check_vma=False
    )
```

```python
import math

import jax
import jax.numpy as jnp
import numpy as np
from jax import lax
from jax.experimental import pallas as pl
from jax.experimental.pallas import tpu as pltpu
from jax.sharding import PartitionSpec as P

F = 16
KC = 128
SUB = 256
R_DEV = 32
SUB_DEV = 2
SUPPORT = 8
NOVER = 256
CHIP = 2 * R_DEV
LANES = 128
BLOCK = 1024
UNROLL = 4

TWO_PI = 2.0 * math.pi

VMEM = pl.BlockSpec(memory_space=pltpu.VMEM)
SMEM = pl.BlockSpec(memory_space=pltpu.SMEM)


def transform_table():
    kcol = np.arange(KC)
    jcol = np.arange(SUB)
    angles = np.float32(TWO_PI) * (kcol[:, None] * jcol[None, :] % SUB).astype(np.float32) / np.float32(SUB)
    scale = np.float32(1.0 / math.sqrt(KC))
    real_part = (np.cos(angles) * scale).astype(jnp.bfloat16)
    imag_part = (np.sin(angles) * scale).astype(jnp.bfloat16)
    upper = np.concatenate([real_part, imag_part], axis=1)
    lower = np.concatenate([-imag_part, real_part], axis=1)
    return np.ascontiguousarray(np.concatenate([upper, lower], axis=0).T)


SHIFTS = (1, 2, -2, -1)


def facet_kernel(devices, start_ref, length_ref, offset_ref, window_ref, rows_ref, *rest, other):
    if other:
        earlier, outs, padded = rest[:5], rest[5:10], rest[10]
    else:
        earlier, outs, padded = None, rest[:5], rest[5]
    total_rows = devices * R_DEV
    chips = devices // 2
    position = lax.axis_index("row")
    chip = position // 2
    core = position % 2
    half = 1 - core if other else core
    base = chip * CHIP + half * R_DEV
    padded[:R_DEV, :] = jnp.zeros((R_DEV, F), jnp.float32)
    padded[R_DEV + SUB :, :] = jnp.zeros((R_DEV, F), jnp.float32)
    padded[R_DEV : R_DEV + SUB, :] = jnp.transpose(window_ref[...])
    row_index = lax.broadcasted_iota(jnp.int32, (R_DEV, F), 0)
    turns = (offset_ref[...] * (base + row_index)) & (total_rows - 1)
    angles = TWO_PI * turns.astype(jnp.float32) / total_rows
    cosines = jnp.cos(angles)
    sines = jnp.sin(angles)
    weights = []
    for shift in (0,) + SHIFTS:
        target = (chip + chips + shift) % chips
        for sub in range(SUB_DEV):
            subgrid = (target * 2 + core) * SUB_DEV + sub
            slot = (base - start_ref[subgrid]) & (total_rows - 1)
            slot = jnp.where(slot > total_rows - R_DEV, slot - total_rows, slot)
            slot = jnp.minimum(slot, SUB)
            piece = padded[pl.ds(slot + R_DEV, R_DEV), :]
            weights.append(jnp.where(slot + row_index < length_ref[subgrid], piece, 0.0))
    for tile in range(R_DEV // 16):
        rows = slice(16 * tile, 16 * tile + 16)
        sums = [[None, None] for _ in weights]
        for f in range(F):
            real_in = rows_ref[0, f, rows, :].astype(jnp.float32)
            imag_in = rows_ref[1, f, rows, :].astype(jnp.float32)
            cos_f = cosines[rows, f : f + 1]
            sin_f = sines[rows, f : f + 1]
            real_part = cos_f * real_in - sin_f * imag_in
            imag_part = cos_f * imag_in + sin_f * real_in
            for entry, weight in zip(sums, weights):
                w = jnp.broadcast_to(weight[rows, f : f + 1], (16, KC))
                entry[0] = w * real_part if f == 0 else entry[0] + w * real_part
                entry[1] = w * imag_part if f == 0 else entry[1] + w * imag_part
        for place, entry in enumerate(sums):
            out, sub = outs[place // SUB_DEV], place % SUB_DEV
            if other:
                first = pl.multiple_of(sub * CHIP + half * R_DEV + 16 * tile, 16)
            else:
                first = sub * R_DEV + 16 * tile
            out[pl.ds(first, 16), :KC] = entry[0].astype(jnp.bfloat16)
            out[pl.ds(first, 16), KC:] = entry[1].astype(jnp.bfloat16)
    if other:
        for piece, out in zip(earlier, outs):
            for sub in range(SUB_DEV):
                first = pl.multiple_of(sub * CHIP + core * R_DEV, R_DEV)
                out[pl.ds(first, R_DEV), :] = piece[sub * R_DEV : (sub + 1) * R_DEV, :]


def taps(low, high, cell, table_row):
    count = cell.shape[1]
    cell = jnp.broadcast_to(cell, (SUPPORT, count))
    table_row = jnp.broadcast_to(table_row, (SUPPORT, count))
    place = table_row & (LANES - 1)
    picked = []
    for first in range(0, count, LANES):
        index = place[:, first : first + LANES]
        from_low = jnp.take_along_axis(low, index, axis=1, mode="promise_in_bounds")
        from_high = jnp.take_along_axis(high, index, axis=1, mode="promise_in_bounds")
        picked.append(jnp.where(table_row[:, first : first + LANES] < LANES, from_low, from_high))
    weights = jnp.concatenate(picked, axis=1)
    for bit in range(3):
        turned = pltpu.roll(weights, 1 << bit, axis=0)
        weights = jnp.where((cell & (1 << bit)) != 0, turned, weights)
    sublane = lax.broadcasted_iota(jnp.int32, (SUPPORT, count), 0)
    tile = (cell >> 3) + jnp.where(sublane < (cell & 7), 1, 0)
    return weights, tile


def degrid_kernel(
    devices,
    per_dest,
    start_ref,
    table_ref,
    transform_ref,
    own_ref,
    below_ref,
    far_below_ref,
    far_above_ref,
    above_ref,
    row_ref,
    column_ref,
    row_kernel_ref,
    column_kernel_ref,
    out_ref,
    cells,
    gathered,
):
    position = lax.axis_index("row")
    chip = position // 2
    table = table_ref[...]
    near = table.astype(jnp.bfloat16).astype(jnp.float32)
    near_low, near_high = near[:, :LANES], near[:, LANES:]
    table_low, table_high = table[:, :LANES], table[:, LANES:]
    for sub in range(SUB_DEV):
        rows = slice(sub * CHIP, sub * CHIP + CHIP)
        summed = jnp.concatenate(
            [
                own_ref[rows, :],
                above_ref[rows, :],
                far_below_ref[rows, :] + far_above_ref[rows, :],
                below_ref[rows, :],
            ],
            axis=0,
        )
        cells[sub] = lax.dot_general(
            transform_ref[...], summed, (((1,), (1,)), ((), ())), preferred_element_type=jnp.float32
        ).astype(jnp.bfloat16)

    chunks = per_dest // LANES

    def one_block(block, carry):
        lanes = pl.ds(pl.multiple_of(block * BLOCK, BLOCK), BLOCK)
        for sub in range(SUB_DEV):
            subgrid = position * SUB_DEV + sub
            shift = start_ref[subgrid] - chip * CHIP
            cell_row = (row_ref[sub : sub + 1, lanes] + shift) & (SUB - 1)
            weights, tile = taps(near_low, near_high, cell_row, row_kernel_ref[sub : sub + 1, lanes])
            tile = tile & (SUB // 8 - 1)
            odd = (tile & 1) != 0
            pair = (tile >> 1).astype(jnp.float32)
            pairs = jnp.concatenate(
                [jnp.where(odd, -1.0, pair), jnp.where(odd, pair, -1.0)], axis=0
            ).astype(jnp.bfloat16)
            both = jnp.concatenate([weights, weights], axis=0).astype(jnp.bfloat16)
            zero = jnp.zeros_like(both)
            spread = jnp.concatenate(
                [jnp.where(pairs == jnp.bfloat16(t), both, zero) for t in range(SUB // 16)], axis=0
            )
            along = jnp.dot(cells[sub], spread, preferred_element_type=jnp.float32)
            weights, tile = taps(
                table_low, table_high, column_ref[sub : sub + 1, lanes], column_kernel_ref[sub : sub + 1, lanes]
            )
            real_part = along[:8]
            imag_part = along[SUB : SUB + 8]
            for t in range(1, SUB // 8):
                here = tile == t
                real_part = jnp.where(here, along[8 * t : 8 * t + 8], real_part)
                imag_part = jnp.where(here, along[SUB + 8 * t : SUB + 8 * t + 8], imag_part)
            sums = [
                jnp.sum(weights * real_part, axis=0, keepdims=True),
                jnp.sum(weights * imag_part, axis=0, keepdims=True),
            ]
            first = block * (BLOCK // LANES * 4)
            for part in range(2):
                for place in range(BLOCK // LANES):
                    row = place // chunks * 4 * chunks + (sub * 2 + part) * chunks + place % chunks
                    gathered[pl.ds(first + row, 1), :] = sums[part][:, place * LANES : (place + 1) * LANES]
        return carry

    lax.fori_loop(0, row_ref.shape[1] // BLOCK, one_block, 0, unroll=UNROLL)
    out_ref[...] = gathered[...].astype(jnp.bfloat16)


def place_kernel(devices, chunks, in_ref, out_ref, wide):
    wide[...] = in_ref[...].astype(jnp.float32)
    for part in range(2):
        for chunk in range(chunks):
            out_ref[part, :, chunk * LANES : (chunk + 1) * LANES] = wide[
                pl.ds(part * chunks + chunk, devices * SUB_DEV, stride=2 * chunks), :
            ]


def local(
    facet_rows,
    range_start,
    range_length,
    facet_offset,
    window_table,
    kernel_table,
    cell_row,
    cell_column,
    kernel_row,
    kernel_column,
):
    devices = lax.axis_size("row")
    chips = devices // 2
    slots = cell_row.shape[1]
    per_dest = slots // devices
    chunks = per_dest // LANES
    other_rows = lax.ppermute(facet_rows, "row", [(i, i ^ 1) for i in range(devices)])
    small = pltpu.CompilerParams(vmem_limit_bytes=8 * 1024 * 1024)
    tables = (range_start, range_length, facet_offset.reshape(1, F), window_table)
    own_pieces = pl.pallas_call(
        lambda *refs: facet_kernel(devices, *refs, other=False),
        out_shape=[jax.ShapeDtypeStruct((SUB_DEV * R_DEV, 2 * KC), jnp.bfloat16)] * 5,
        in_specs=[SMEM, SMEM, VMEM, VMEM, VMEM],
        out_specs=[VMEM] * 5,
        scratch_shapes=[pltpu.VMEM((SUB + 2 * R_DEV, F), jnp.float32)],
        compiler_params=small,
        name="own_facet_sums",
    )(*tables, facet_rows)
    pieces = pl.pallas_call(
        lambda *refs: facet_kernel(devices, *refs, other=True),
        out_shape=[jax.ShapeDtypeStruct((SUB_DEV * CHIP, 2 * KC), jnp.bfloat16)] * 5,
        in_specs=[SMEM, SMEM] + [VMEM] * 8,
        out_specs=[VMEM] * 5,
        scratch_shapes=[pltpu.VMEM((SUB + 2 * R_DEV, F), jnp.float32)],
        compiler_params=small,
        name="other_facet_sums",
    )(*tables, other_rows, *own_pieces)
    came = []
    for shift, piece in zip(SHIFTS, pieces[1:]):
        pairs = [
            (2 * chip + core, 2 * ((chip + shift) % chips) + core)
            for chip in range(chips)
            for core in range(2)
        ]
        came.append(lax.ppermute(piece, "row", pairs))
    rows_out = devices * 4 * chunks
    results = pl.pallas_call(
        lambda *refs: degrid_kernel(devices, per_dest, *refs),
        out_shape=jax.ShapeDtypeStruct((rows_out, LANES), jnp.bfloat16),
        in_specs=[SMEM] + [VMEM] * 11,
        out_specs=VMEM,
        scratch_shapes=[
            pltpu.VMEM((SUB_DEV, 2 * SUB, SUB), jnp.bfloat16),
            pltpu.VMEM((rows_out, LANES), jnp.float32),
        ],
        compiler_params=pltpu.CompilerParams(vmem_limit_bytes=32 * 1024 * 1024),
        name="degrid",
    )(
        range_start,
        kernel_table.T,
        jnp.asarray(transform_table()),
        pieces[0],
        *came,
        cell_row,
        cell_column,
        kernel_row,
        kernel_column,
    )
    received = lax.all_to_all(
        results.reshape(devices, 4 * chunks, LANES), "row", split_axis=0, concat_axis=0, tiled=True
    )
    return pl.pallas_call(
        lambda *refs: place_kernel(devices, chunks, *refs),
        out_shape=jax.ShapeDtypeStruct((2, devices * SUB_DEV, per_dest), jnp.float32),
        in_specs=[VMEM],
        out_specs=VMEM,
        scratch_shapes=[pltpu.VMEM((rows_out, LANES), jnp.float32)],
        compiler_params=small,
        name="place",
    )(received.reshape(rows_out, LANES))


def solution(mesh):
    placed = (
        P(None, None, ("grp", "row"), None),
        P("grp"),
        P("grp"),
        P("grp"),
        P(),
        P(),
        P(("grp", "row"), None),
        P(("grp", "row"), None),
        P(("grp", "row"), None),
        P(("grp", "row"), None),
    )
    return jax.shard_map(
        local, mesh=mesh, in_specs=placed, out_specs=P(None, "grp", "row"), check_vma=False
    )
```

```python
import math

import jax
import jax.numpy as jnp
import numpy as np
from jax import lax
from jax.experimental import pallas as pl
from jax.experimental.pallas import tpu as pltpu
from jax.sharding import PartitionSpec as P

F = 16
KC = 128
SUB = 256
R_DEV = 32
SUB_DEV = 2
SUPPORT = 8
NOVER = 256
CHIP = 2 * R_DEV
LANES = 128
BLOCK = 1024
UNROLL = 4

TWO_PI = 2.0 * math.pi

VMEM = pl.BlockSpec(memory_space=pltpu.VMEM)
HBM = pl.BlockSpec(memory_space=pltpu.HBM)


def transform_table():
    kcol = np.arange(KC)
    jcol = np.arange(SUB)
    angles = np.float32(TWO_PI) * (kcol[:, None] * jcol[None, :] % SUB).astype(np.float32) / np.float32(SUB)
    scale = np.float32(1.0 / math.sqrt(KC))
    real_part = (np.cos(angles) * scale).astype(jnp.bfloat16)
    imag_part = (np.sin(angles) * scale).astype(jnp.bfloat16)
    upper = np.concatenate([real_part, imag_part], axis=1)
    lower = np.concatenate([-imag_part, real_part], axis=1)
    return np.ascontiguousarray(np.concatenate([upper, lower], axis=0).T)


SHIFTS = (1, 2, -2, -1)


def facet_products(factors, rows_ref, outs, half_step, first_row):
    for group in range(R_DEV // 16):
        rows = slice(16 * group, 16 * group + 16)
        cells = jnp.concatenate(
            [rows_ref[0, :, rows, :].reshape(F * 16, KC), rows_ref[1, :, rows, :].reshape(F * 16, KC)], axis=1
        )
        products = []
        for kind in range(2):
            high = jnp.dot(factors(group, 2 * kind), cells, preferred_element_type=jnp.float32)
            low = jnp.dot(factors(group, 2 * kind + 1), cells, preferred_element_type=jnp.float32)
            products.append(high + low)
        with_cos, with_sin = products
        real_part = (with_cos[:, :KC] - with_sin[:, KC:]).astype(jnp.bfloat16)
        imag_part = (with_cos[:, KC:] + with_sin[:, :KC]).astype(jnp.bfloat16)
        for place, out in enumerate(outs):
            for sub in range(SUB_DEV):
                here = slice((place * SUB_DEV + sub) * 16, (place * SUB_DEV + sub) * 16 + 16)
                first = first_row + sub * half_step + 16 * group
                if not isinstance(first, int):
                    first = pl.multiple_of(first, 16)
                out[pl.ds(first, 16), :KC] = real_part[here]
                out[pl.ds(first, 16), KC:] = imag_part[here]


def own_facet_kernel(
    devices,
    start_hbm,
    length_hbm,
    offset_hbm,
    window_hbm,
    rows_hbm,
    *rest,
):
    outs, other_factors, shifts = rest[:5], rest[5], rest[6]
    start, length, offset, window, rows_ref, own_factors, padded, sems = rest[7:]
    copies = [
        pltpu.make_async_copy(source, target, sems.at[number])
        for number, (source, target) in enumerate(
            (
                (start_hbm, start),
                (length_hbm, length),
                (offset_hbm, offset),
                (window_hbm, window),
                (rows_hbm, rows_ref),
            )
        )
    ]
    for copy in copies:
        copy.start()
    total_rows = devices * R_DEV
    chips = devices // 2
    position = lax.axis_index("row")
    chip = position // 2
    core = position % 2
    padded[:R_DEV, :] = jnp.zeros((R_DEV, F), jnp.float32)
    padded[R_DEV + SUB :, :] = jnp.zeros((R_DEV, F), jnp.float32)
    row_index = lax.broadcasted_iota(jnp.int32, (R_DEV, F), 0)
    lane = lax.broadcasted_iota(jnp.int32, (R_DEV, LANES), 1)
    sublane = lax.broadcasted_iota(jnp.int32, (R_DEV, LANES), 0)
    diagonal = (lane & 15) == (sublane & 15)

    def spread(values):
        wide = jnp.concatenate([values, jnp.zeros((R_DEV, LANES - F), values.dtype)], axis=1)
        return [
            jnp.concatenate(
                [
                    jnp.take_along_axis(
                        wide[row : row + 8], (lane[:8] >> 4) + 8 * side, axis=1, mode="promise_in_bounds"
                    )
                    for row in range(0, R_DEV, 8)
                ],
                axis=0,
            )
            for side in range(2)
        ]

    for copy in copies[:4]:
        copy.wait()
    padded[R_DEV : R_DEV + SUB, :] = jnp.transpose(window[...])
    for sub in range(SUB_DEV):
        shift = start[position * SUB_DEV + sub] - chip * CHIP
        shifts[sub] = jnp.full((8, LANES), shift, jnp.int32)
    for held, factors in enumerate((own_factors, other_factors)):
        half = core if held == 0 else 1 - core
        base = chip * CHIP + half * R_DEV
        turns = (offset[...] * (base + row_index)) & (total_rows - 1)
        angles = TWO_PI * turns.astype(jnp.float32) / total_rows
        phases = [
            [jnp.where(diagonal, side, 0.0) for side in spread(part)]
            for part in (jnp.cos(angles), jnp.sin(angles))
        ]
        for place, shift in enumerate((0,) + SHIFTS):
            target = (chip + chips + shift) % chips
            for sub in range(SUB_DEV):
                subgrid = (target * 2 + core) * SUB_DEV + sub
                slot = (base - start[subgrid]) & (total_rows - 1)
                slot = jnp.where(slot > total_rows - R_DEV, slot - total_rows, slot)
                slot = jnp.minimum(slot, SUB)
                piece = padded[pl.ds(slot + R_DEV, R_DEV), :]
                weights = spread(jnp.where(slot + row_index < length[subgrid], piece, 0.0))
                for kind in range(2):
                    for side in range(2):
                        exact = weights[side] * phases[kind][side]
                        high = exact.astype(jnp.bfloat16)
                        low = (exact - high.astype(jnp.float32)).astype(jnp.bfloat16)
                        lanes = slice(side * LANES, (side + 1) * LANES)
                        for group in range(R_DEV // 16):
                            rows = slice(16 * group, 16 * group + 16)
                            here = slice((place * SUB_DEV + sub) * 16, (place * SUB_DEV + sub) * 16 + 16)
                            factors[group, 2 * kind, here, lanes] = high[rows]
                            factors[group, 2 * kind + 1, here, lanes] = low[rows]
    copies[4].wait()
    facet_products(lambda group, kind: own_factors[group, kind], rows_ref, outs, R_DEV, 0)


def other_facet_kernel(rows_ref, factors, *rest):
    earlier, outs = rest[:5], rest[5:]
    core = lax.axis_index("row") % 2
    for piece, out in zip(earlier, outs):
        for sub in range(SUB_DEV):
            first = pl.multiple_of(sub * CHIP + core * R_DEV, R_DEV)
            out[pl.ds(first, R_DEV), :] = piece[sub * R_DEV : (sub + 1) * R_DEV, :]
    facet_products(lambda group, kind: factors[group, kind], rows_ref, outs, CHIP, (1 - core) * R_DEV)


def taps(low, high, cell, table_row):
    count = cell.shape[1]
    cell = jnp.broadcast_to(cell, (SUPPORT, count))
    table_row = jnp.broadcast_to(table_row, (SUPPORT, count))
    place = table_row & (LANES - 1)
    picked = []
    for first in range(0, count, LANES):
        index = place[:, first : first + LANES]
        from_low = jnp.take_along_axis(low, index, axis=1, mode="promise_in_bounds")
        from_high = jnp.take_along_axis(high, index, axis=1, mode="promise_in_bounds")
        picked.append(jnp.where(table_row[:, first : first + LANES] < LANES, from_low, from_high))
    weights = jnp.concatenate(picked, axis=1)
    for bit in range(3):
        turned = pltpu.roll(weights, 1 << bit, axis=0)
        weights = jnp.where((cell & (1 << bit)) != 0, turned, weights)
    sublane = lax.broadcasted_iota(jnp.int32, (SUPPORT, count), 0)
    tile = (cell >> 3) + jnp.where(sublane < (cell & 7), 1, 0)
    return weights, tile


def degrid_kernel(
    devices,
    per_dest,
    shifts_ref,
    table_ref,
    transform_ref,
    own_ref,
    below_ref,
    far_below_ref,
    far_above_ref,
    above_ref,
    row_ref,
    column_ref,
    row_kernel_ref,
    column_kernel_ref,
    out_ref,
    cells,
    gathered,
):
    table = table_ref[...]
    near = table.astype(jnp.bfloat16).astype(jnp.float32)
    near_low, near_high = near[:, :LANES], near[:, LANES:]
    table_low, table_high = table[:, :LANES], table[:, LANES:]
    for sub in range(SUB_DEV):
        rows = slice(sub * CHIP, sub * CHIP + CHIP)
        summed = jnp.concatenate(
            [
                own_ref[rows, :],
                above_ref[rows, :],
                far_below_ref[rows, :] + far_above_ref[rows, :],
                below_ref[rows, :],
            ],
            axis=0,
        )
        cells[sub] = lax.dot_general(
            transform_ref[...], summed, (((1,), (1,)), ((), ())), preferred_element_type=jnp.float32
        ).astype(jnp.bfloat16)

    chunks = per_dest // LANES

    def one_block(block, carry):
        lanes = pl.ds(pl.multiple_of(block * BLOCK, BLOCK), BLOCK)
        for sub in range(SUB_DEV):
            shift = jnp.concatenate([shifts_ref[sub, :1, :]] * (BLOCK // LANES), axis=1)
            cell_row = (row_ref[sub : sub + 1, lanes] + shift) & (SUB - 1)
            weights, tile = taps(near_low, near_high, cell_row, row_kernel_ref[sub : sub + 1, lanes])
            tile = tile & (SUB // 8 - 1)
            odd = (tile & 1) != 0
            pair = (tile >> 1).astype(jnp.float32)
            pairs = jnp.concatenate(
                [jnp.where(odd, -1.0, pair), jnp.where(odd, pair, -1.0)], axis=0
            ).astype(jnp.bfloat16)
            both = jnp.concatenate([weights, weights], axis=0).astype(jnp.bfloat16)
            zero = jnp.zeros_like(both)
            spread = jnp.concatenate(
                [jnp.where(pairs == jnp.bfloat16(t), both, zero) for t in range(SUB // 16)], axis=0
            )
            along = jnp.dot(cells[sub], spread, preferred_element_type=jnp.float32)
            weights, tile = taps(
                table_low, table_high, column_ref[sub : sub + 1, lanes], column_kernel_ref[sub : sub + 1, lanes]
            )
            real_part = along[:8]
            imag_part = along[SUB : SUB + 8]
            for t in range(1, SUB // 8):
                here = tile == t
                real_part = jnp.where(here, along[8 * t : 8 * t + 8], real_part)
                imag_part = jnp.where(here, along[SUB + 8 * t : SUB + 8 * t + 8], imag_part)
            sums = [
                jnp.sum(weights * real_part, axis=0, keepdims=True),
                jnp.sum(weights * imag_part, axis=0, keepdims=True),
            ]
            first = block * (BLOCK // LANES * 4)
            for part in range(2):
                for place in range(BLOCK // LANES):
                    row = place // chunks * 4 * chunks + (sub * 2 + part) * chunks + place % chunks
                    gathered[pl.ds(first + row, 1), :] = sums[part][:, place * LANES : (place + 1) * LANES]
        return carry

    lax.fori_loop(0, row_ref.shape[1] // BLOCK, one_block, 0, unroll=UNROLL)
    out_ref[...] = gathered[...].astype(jnp.bfloat16)


def place_kernel(devices, chunks, in_ref, out_ref, wide):
    wide[...] = in_ref[...].astype(jnp.float32)
    for part in range(2):
        for chunk in range(chunks):
            out_ref[part, :, chunk * LANES : (chunk + 1) * LANES] = wide[
                pl.ds(part * chunks + chunk, devices * SUB_DEV, stride=2 * chunks), :
            ]


def local(
    facet_rows,
    range_start,
    range_length,
    facet_offset,
    window_table,
    kernel_table,
    cell_row,
    cell_column,
    kernel_row,
    kernel_column,
):
    devices = lax.axis_size("row")
    chips = devices // 2
    slots = cell_row.shape[1]
    per_dest = slots // devices
    chunks = per_dest // LANES
    other_rows = lax.ppermute(facet_rows, "row", [(i, i ^ 1) for i in range(devices)])
    small = pltpu.CompilerParams(vmem_limit_bytes=12 * 1024 * 1024)
    factors = jax.ShapeDtypeStruct((R_DEV // 16, 4, 5 * SUB_DEV * 16, 16 * F), jnp.bfloat16)
    *own_pieces, other_factors, shifts = pl.pallas_call(
        lambda *refs: own_facet_kernel(devices, *refs),
        out_shape=[jax.ShapeDtypeStruct((SUB_DEV * R_DEV, 2 * KC), jnp.bfloat16)] * 5
        + [factors, jax.ShapeDtypeStruct((SUB_DEV, 8, LANES), jnp.int32)],
        in_specs=[HBM] * 5,
        out_specs=[VMEM] * 7,
        scratch_shapes=[
            pltpu.SMEM(range_start.shape, jnp.int32),
            pltpu.SMEM(range_length.shape, jnp.int32),
            pltpu.VMEM((1, F), jnp.int32),
            pltpu.VMEM(window_table.shape, jnp.float32),
            pltpu.VMEM(facet_rows.shape, jnp.bfloat16),
            pltpu.VMEM(factors.shape, jnp.bfloat16),
            pltpu.VMEM((SUB + 2 * R_DEV, F), jnp.float32),
            pltpu.SemaphoreType.DMA((5,)),
        ],
        compiler_params=small,
        name="own_facet_sums",
    )(
        *(
            pltpu.with_memory_space_constraint(value, pltpu.HBM)
            for value in (range_start, range_length, facet_offset.reshape(1, F), window_table, facet_rows)
        )
    )
    pieces = pl.pallas_call(
        other_facet_kernel,
        out_shape=[jax.ShapeDtypeStruct((SUB_DEV * CHIP, 2 * KC), jnp.bfloat16)] * 5,
        in_specs=[VMEM] * 7,
        out_specs=[VMEM] * 5,
        compiler_params=small,
        name="other_facet_sums",
    )(other_rows, other_factors, *own_pieces)
    came = []
    for shift, piece in zip(SHIFTS, pieces[1:]):
        pairs = [
            (2 * chip + core, 2 * ((chip + shift) % chips) + core)
            for chip in range(chips)
            for core in range(2)
        ]
        came.append(lax.ppermute(piece, "row", pairs))
    rows_out = devices * 4 * chunks
    results = pl.pallas_call(
        lambda *refs: degrid_kernel(devices, per_dest, *refs),
        out_shape=jax.ShapeDtypeStruct((rows_out, LANES), jnp.bfloat16),
        in_specs=[VMEM] * 12,
        out_specs=VMEM,
        scratch_shapes=[
            pltpu.VMEM((SUB_DEV, 2 * SUB, SUB), jnp.bfloat16),
            pltpu.VMEM((rows_out, LANES), jnp.float32),
        ],
        compiler_params=pltpu.CompilerParams(vmem_limit_bytes=32 * 1024 * 1024),
        name="degrid",
    )(
        shifts,
        kernel_table.T,
        jnp.asarray(transform_table()),
        pieces[0],
        *came,
        cell_row,
        cell_column,
        kernel_row,
        kernel_column,
    )
    received = lax.all_to_all(
        results.reshape(devices, 4 * chunks, LANES), "row", split_axis=0, concat_axis=0, tiled=True
    )
    return pl.pallas_call(
        lambda *refs: place_kernel(devices, chunks, *refs),
        out_shape=jax.ShapeDtypeStruct((2, devices * SUB_DEV, per_dest), jnp.float32),
        in_specs=[VMEM],
        out_specs=VMEM,
        scratch_shapes=[pltpu.VMEM((rows_out, LANES), jnp.float32)],
        compiler_params=small,
        name="place",
    )(received.reshape(rows_out, LANES))


def solution(mesh):
    placed = (
        P(None, None, ("grp", "row"), None),
        P("grp"),
        P("grp"),
        P("grp"),
        P(),
        P(),
        P(("grp", "row"), None),
        P(("grp", "row"), None),
        P(("grp", "row"), None),
        P(("grp", "row"), None),
    )
    return jax.shard_map(
        local, mesh=mesh, in_specs=placed, out_specs=P(None, "grp", "row"), check_vma=False
    )
```

```python
import math

import jax
import jax.numpy as jnp
import numpy as np
from jax import lax
from jax.experimental import pallas as pl
from jax.experimental.pallas import tpu as pltpu
from jax.sharding import PartitionSpec as P

F = 16
KC = 128
SUB = 256
R_DEV = 32
SUB_DEV = 2
SUPPORT = 8
NOVER = 256
CHIP = 2 * R_DEV
LANES = 128
BLOCK = 1024
UNROLL = 4
PART = 512
PART_UNROLL = 8

TWO_PI = 2.0 * math.pi

VMEM = pl.BlockSpec(memory_space=pltpu.VMEM)
HBM = pl.BlockSpec(memory_space=pltpu.HBM)


def turned_rows():
    wave = np.arange(KC)
    place = wave // 8 * 16 + wave % 8
    return np.concatenate([place, place + 8])


def transform_table():
    kcol = np.arange(KC)
    jcol = np.arange(SUB)
    angles = np.float32(TWO_PI) * (kcol[:, None] * jcol[None, :] % SUB).astype(np.float32) / np.float32(SUB)
    scale = np.float32(1.0 / math.sqrt(KC))
    parts = np.concatenate([np.cos(angles) * scale, np.sin(angles) * scale], axis=0).astype(jnp.bfloat16)
    table = np.zeros_like(parts)
    table[turned_rows()] = parts
    return table


SHIFTS = (1, 2, -2, -1)
LATER = 6


def facet_products(factors, rows_ref, outs, half_step, first_row):
    for group in range(R_DEV // 16):
        rows = slice(16 * group, 16 * group + 16)
        cells = jnp.concatenate(
            [rows_ref[0, :, rows, :].reshape(F * 16, KC), rows_ref[1, :, rows, :].reshape(F * 16, KC)], axis=1
        )
        products = []
        for kind in range(2):
            high = jnp.dot(factors(group, 2 * kind), cells, preferred_element_type=jnp.float32)
            low = jnp.dot(factors(group, 2 * kind + 1), cells, preferred_element_type=jnp.float32)
            products.append(high + low)
        with_cos, with_sin = products
        real_part = (with_cos[:, :KC] - with_sin[:, KC:]).astype(jnp.bfloat16)
        imag_part = (with_cos[:, KC:] + with_sin[:, :KC]).astype(jnp.bfloat16)
        for place, out in enumerate(outs):
            for sub in range(SUB_DEV):
                here = slice((place * SUB_DEV + sub) * 16, (place * SUB_DEV + sub) * 16 + 16)
                first = first_row + sub * half_step + 16 * group
                if not isinstance(first, int):
                    first = pl.multiple_of(first, 16)
                out[pl.ds(first, 16), :KC] = real_part[here]
                out[pl.ds(first, 16), KC:] = imag_part[here]


def own_facet_kernel(
    devices,
    start_hbm,
    length_hbm,
    offset_hbm,
    window_hbm,
    rows_hbm,
    *rest,
):
    later_hbm, rest = rest[:LATER], rest[LATER:]
    outs, other_factors, shifts, later = rest[:5], rest[5], rest[6], rest[7 : 7 + LATER]
    start, length, offset, window, rows_ref, own_factors, padded, sems = rest[7 + LATER :]
    copies = [
        pltpu.make_async_copy(source, target, sems.at[number])
        for number, (source, target) in enumerate(
            (
                (start_hbm, start),
                (length_hbm, length),
                (offset_hbm, offset),
                (window_hbm, window),
                (rows_hbm, rows_ref),
                *zip(later_hbm, later),
            )
        )
    ]
    for copy in copies:
        copy.start()
    total_rows = devices * R_DEV
    chips = devices // 2
    position = lax.axis_index("row")
    chip = position // 2
    core = position % 2
    padded[:R_DEV, :] = jnp.zeros((R_DEV, F), jnp.float32)
    padded[R_DEV + SUB :, :] = jnp.zeros((R_DEV, F), jnp.float32)
    row_index = lax.broadcasted_iota(jnp.int32, (R_DEV, F), 0)
    lane = lax.broadcasted_iota(jnp.int32, (R_DEV, LANES), 1)
    sublane = lax.broadcasted_iota(jnp.int32, (R_DEV, LANES), 0)
    diagonal = (lane & 15) == (sublane & 15)

    def spread(values):
        wide = jnp.concatenate([values, jnp.zeros((R_DEV, LANES - F), values.dtype)], axis=1)
        return [
            jnp.concatenate(
                [
                    jnp.take_along_axis(
                        wide[row : row + 8], (lane[:8] >> 4) + 8 * side, axis=1, mode="promise_in_bounds"
                    )
                    for row in range(0, R_DEV, 8)
                ],
                axis=0,
            )
            for side in range(2)
        ]

    for copy in copies[:4]:
        copy.wait()
    padded[R_DEV : R_DEV + SUB, :] = jnp.transpose(window[...])
    for sub in range(SUB_DEV):
        shift = start[position * SUB_DEV + sub] - chip * CHIP
        shifts[sub] = jnp.full((8, LANES), shift, jnp.int32)
    for held, factors in enumerate((own_factors, other_factors)):
        half = core if held == 0 else 1 - core
        base = chip * CHIP + half * R_DEV
        turns = (offset[...] * (base + row_index)) & (total_rows - 1)
        angles = TWO_PI * turns.astype(jnp.float32) / total_rows
        phases = [
            [jnp.where(diagonal, side, 0.0) for side in spread(part)]
            for part in (jnp.cos(angles), jnp.sin(angles))
        ]
        for place, shift in enumerate((0,) + SHIFTS):
            target = (chip + chips + shift) % chips
            for sub in range(SUB_DEV):
                subgrid = (target * 2 + core) * SUB_DEV + sub
                slot = (base - start[subgrid]) & (total_rows - 1)
                slot = jnp.where(slot > total_rows - R_DEV, slot - total_rows, slot)
                slot = jnp.minimum(slot, SUB)
                piece = padded[pl.ds(slot + R_DEV, R_DEV), :]
                weights = spread(jnp.where(slot + row_index < length[subgrid], piece, 0.0))
                for kind in range(2):
                    for side in range(2):
                        exact = weights[side] * phases[kind][side]
                        high = exact.astype(jnp.bfloat16)
                        low = (exact - high.astype(jnp.float32)).astype(jnp.bfloat16)
                        lanes = slice(side * LANES, (side + 1) * LANES)
                        for group in range(R_DEV // 16):
                            rows = slice(16 * group, 16 * group + 16)
                            here = slice((place * SUB_DEV + sub) * 16, (place * SUB_DEV + sub) * 16 + 16)
                            factors[group, 2 * kind, here, lanes] = high[rows]
                            factors[group, 2 * kind + 1, here, lanes] = low[rows]
    copies[4].wait()
    facet_products(lambda group, kind: own_factors[group, kind], rows_ref, outs, R_DEV, 0)
    for copy in copies[5:]:
        copy.wait()


def other_facet_kernel(rows_ref, factors, shifts, *rest):
    earlier, outs, shifts_out = rest[:5], rest[5:10], rest[10]
    shifts_out[...] = shifts[...]
    core = lax.axis_index("row") % 2
    for piece, out in zip(earlier, outs):
        for sub in range(SUB_DEV):
            first = pl.multiple_of(sub * CHIP + core * R_DEV, R_DEV)
            out[pl.ds(first, R_DEV), :] = piece[sub * R_DEV : (sub + 1) * R_DEV, :]
    facet_products(lambda group, kind: factors[group, kind], rows_ref, outs, CHIP, (1 - core) * R_DEV)


def spread(low, high, cell, table_row):
    count = cell.shape[1]
    cell = jnp.broadcast_to(cell, (SUPPORT, count))
    table_row = jnp.broadcast_to(table_row, (SUPPORT, count))
    place = table_row & (LANES - 1)
    picked = []
    for first in range(0, count, LANES):
        index = place[:, first : first + LANES]
        from_low = jnp.take_along_axis(low, index, axis=1, mode="promise_in_bounds")
        from_high = jnp.take_along_axis(high, index, axis=1, mode="promise_in_bounds")
        picked.append(jnp.where(table_row[:, first : first + LANES] < LANES, from_low, from_high))
    weights = jnp.concatenate(picked, axis=1)
    for bit in range(3):
        turned = pltpu.roll(weights, 1 << bit, axis=0)
        weights = jnp.where((cell & (1 << bit)) != 0, turned, weights)
    sublane = lax.broadcasted_iota(jnp.int32, (SUPPORT, count), 0)
    tile = ((cell >> 3) + jnp.where(sublane < (cell & 7), 1, 0)) & (SUB // 8 - 1)
    odd = (tile & 1) != 0
    pair = (tile >> 1).astype(jnp.float32)
    pairs = jnp.concatenate([jnp.where(odd, -1.0, pair), jnp.where(odd, pair, -1.0)], axis=0).astype(jnp.bfloat16)
    both = jnp.concatenate([weights, weights], axis=0).astype(jnp.bfloat16)
    zero = jnp.zeros_like(both)
    return jnp.concatenate([jnp.where(pairs == jnp.bfloat16(t), both, zero) for t in range(SUB // 16)], axis=0)


def spread_kernel(
    shifts_ref,
    table_ref,
    transform_ref,
    row_ref,
    column_ref,
    row_kernel_ref,
    column_kernel_ref,
    row_spread,
    column_waves,
):
    low, high = table_ref[:, :LANES], table_ref[:, LANES:]

    def one_block(block, carry):
        lanes = pl.ds(pl.multiple_of(block * BLOCK, BLOCK), BLOCK)
        for sub in range(SUB_DEV):
            shift = jnp.concatenate([shifts_ref[sub, :1, :]] * (BLOCK // LANES), axis=1)
            cell_row = (row_ref[sub : sub + 1, lanes] + shift) & (SUB - 1)
            row_spread[sub, :, lanes] = spread(low, high, cell_row, row_kernel_ref[sub : sub + 1, lanes])
            columns = spread(low, high, column_ref[sub : sub + 1, lanes], column_kernel_ref[sub : sub + 1, lanes])
            column_waves[sub, :, lanes] = jnp.dot(transform_ref[...], columns, preferred_element_type=jnp.float32)
        return carry

    lax.fori_loop(0, row_ref.shape[1] // BLOCK, one_block, 0, unroll=UNROLL)


def degrid_kernel(
    per_dest,
    own_ref,
    below_ref,
    far_below_ref,
    far_above_ref,
    above_ref,
    row_spread,
    column_waves,
    out_ref,
    waves,
    gathered,
):
    wave = lax.broadcasted_iota(jnp.int32, (2 * KC, 2 * KC), 1)
    place = ((wave & (KC - 1)) >> 3) * 16 + (wave & 7) + jnp.where(wave < KC, 0, 8)
    turn = (lax.broadcasted_iota(jnp.int32, (2 * KC, 2 * KC), 0) == place).astype(jnp.float32).astype(jnp.bfloat16)
    for sub in range(SUB_DEV):
        rows = slice(sub * CHIP, sub * CHIP + CHIP)
        summed = jnp.concatenate(
            [
                own_ref[rows, :],
                above_ref[rows, :],
                far_below_ref[rows, :] + far_above_ref[rows, :],
                below_ref[rows, :],
            ],
            axis=0,
        )
        waves[sub] = lax.dot_general(
            turn, summed, (((1,), (1,)), ((), ())), preferred_element_type=jnp.float32
        ).astype(jnp.bfloat16)
    chunks = per_dest // LANES

    def one_block(block, carry):
        lanes = pl.ds(pl.multiple_of(block * PART, PART), PART)
        for sub in range(SUB_DEV):
            along = jnp.dot(waves[sub], row_spread[sub, :, lanes], preferred_element_type=jnp.float32)
            sums = [None, None]
            for t in range(KC // 8):
                real = slice(16 * t, 16 * t + 8)
                imag = slice(16 * t + 8, 16 * t + 16)
                real_wave = column_waves[sub, real, lanes]
                imag_wave = column_waves[sub, imag, lanes]
                terms = (
                    along[real] * real_wave - along[imag] * imag_wave,
                    along[real] * imag_wave + along[imag] * real_wave,
                )
                sums = [term if t == 0 else total + term for total, term in zip(sums, terms)]
            first = block * (PART // LANES * 4)
            for part in range(2):
                total = jnp.sum(sums[part], axis=0, keepdims=True)
                for place in range(PART // LANES):
                    row = place // chunks * 4 * chunks + (sub * 2 + part) * chunks + place % chunks
                    gathered[pl.ds(first + row, 1), :] = total[:, place * LANES : (place + 1) * LANES]
        return carry

    lax.fori_loop(0, row_spread.shape[2] // PART, one_block, 0, unroll=PART_UNROLL)
    out_ref[...] = gathered[...].astype(jnp.bfloat16)


def place_kernel(devices, chunks, in_ref, out_ref, wide):
    wide[...] = in_ref[...].astype(jnp.float32)
    for part in range(2):
        for chunk in range(chunks):
            out_ref[part, :, chunk * LANES : (chunk + 1) * LANES] = wide[
                pl.ds(part * chunks + chunk, devices * SUB_DEV, stride=2 * chunks), :
            ]


def local(
    facet_rows,
    range_start,
    range_length,
    facet_offset,
    window_table,
    kernel_table,
    cell_row,
    cell_column,
    kernel_row,
    kernel_column,
):
    devices = lax.axis_size("row")
    chips = devices // 2
    slots = cell_row.shape[1]
    per_dest = slots // devices
    chunks = per_dest // LANES
    other_rows = lax.ppermute(facet_rows, "row", [(i, i ^ 1) for i in range(devices)])
    small = pltpu.CompilerParams(vmem_limit_bytes=12 * 1024 * 1024)
    factors = jax.ShapeDtypeStruct((R_DEV // 16, 4, 5 * SUB_DEV * 16, 16 * F), jnp.bfloat16)
    later = (kernel_table.T, jnp.asarray(transform_table()), cell_row, cell_column, kernel_row, kernel_column)
    *own_pieces, other_factors, shifts, table, transform, rows, columns, row_kernels, column_kernels = pl.pallas_call(
        lambda *refs: own_facet_kernel(devices, *refs),
        out_shape=[jax.ShapeDtypeStruct((SUB_DEV * R_DEV, 2 * KC), jnp.bfloat16)] * 5
        + [factors, jax.ShapeDtypeStruct((SUB_DEV, 8, LANES), jnp.int32)]
        + [jax.ShapeDtypeStruct(value.shape, value.dtype) for value in later],
        in_specs=[HBM] * (5 + LATER),
        out_specs=[VMEM] * (7 + LATER),
        scratch_shapes=[
            pltpu.SMEM(range_start.shape, jnp.int32),
            pltpu.SMEM(range_length.shape, jnp.int32),
            pltpu.VMEM((1, F), jnp.int32),
            pltpu.VMEM(window_table.shape, jnp.float32),
            pltpu.VMEM(facet_rows.shape, jnp.bfloat16),
            pltpu.VMEM(factors.shape, jnp.bfloat16),
            pltpu.VMEM((SUB + 2 * R_DEV, F), jnp.float32),
            pltpu.SemaphoreType.DMA((5 + LATER,)),
        ],
        compiler_params=small,
        name="own_facet_sums",
    )(
        *(
            pltpu.with_memory_space_constraint(value, pltpu.HBM)
            for value in (range_start, range_length, facet_offset.reshape(1, F), window_table, facet_rows, *later)
        )
    )
    *pieces, shifts = pl.pallas_call(
        other_facet_kernel,
        out_shape=[jax.ShapeDtypeStruct((SUB_DEV * CHIP, 2 * KC), jnp.bfloat16)] * 5
        + [jax.ShapeDtypeStruct((SUB_DEV, 8, LANES), jnp.int32)],
        in_specs=[VMEM] * 8,
        out_specs=[VMEM] * 6,
        compiler_params=small,
        name="other_facet_sums",
    )(other_rows, other_factors, shifts, *own_pieces)
    came = []
    for shift, piece in zip(SHIFTS, pieces[1:]):
        pairs = [
            (2 * chip + core, 2 * ((chip + shift) % chips) + core)
            for chip in range(chips)
            for core in range(2)
        ]
        came.append(lax.ppermute(piece, "row", pairs))
    rows_out = devices * 4 * chunks
    spread_shape = (SUB_DEV, SUB, slots)
    row_spread, column_waves = pl.pallas_call(
        spread_kernel,
        out_shape=[
            jax.ShapeDtypeStruct(spread_shape, jnp.bfloat16),
            jax.ShapeDtypeStruct(spread_shape, jnp.float32),
        ],
        in_specs=[VMEM] * 7,
        out_specs=[VMEM] * 2,
        compiler_params=small,
        cost_estimate=pl.CostEstimate(
            flops=2 * SUB_DEV * SUB * 2 * KC * slots, bytes_accessed=6 * SUB_DEV * SUB * slots, transcendentals=0
        ),
        name="spread",
    )(shifts, table, transform, rows, columns, row_kernels, column_kernels)
    results = pl.pallas_call(
        lambda *refs: degrid_kernel(per_dest, *refs),
        out_shape=jax.ShapeDtypeStruct((rows_out, LANES), jnp.bfloat16),
        in_specs=[VMEM] * 7,
        out_specs=VMEM,
        scratch_shapes=[
            pltpu.VMEM((SUB_DEV, 2 * KC, SUB), jnp.bfloat16),
            pltpu.VMEM((rows_out, LANES), jnp.float32),
        ],
        compiler_params=small,
        name="degrid",
    )(pieces[0], *came, row_spread, column_waves)
    received = lax.all_to_all(
        results.reshape(devices, 4 * chunks, LANES), "row", split_axis=0, concat_axis=0, tiled=True
    )
    return pl.pallas_call(
        lambda *refs: place_kernel(devices, chunks, *refs),
        out_shape=jax.ShapeDtypeStruct((2, devices * SUB_DEV, per_dest), jnp.float32),
        in_specs=[VMEM],
        out_specs=VMEM,
        scratch_shapes=[pltpu.VMEM((rows_out, LANES), jnp.float32)],
        compiler_params=small,
        name="place",
    )(received.reshape(rows_out, LANES))


def solution(mesh):
    placed = (
        P(None, None, ("grp", "row"), None),
        P("grp"),
        P("grp"),
        P("grp"),
        P(),
        P(),
        P(("grp", "row"), None),
        P(("grp", "row"), None),
        P(("grp", "row"), None),
        P(("grp", "row"), None),
    )
    return jax.shard_map(
        local, mesh=mesh, in_specs=placed, out_specs=P(None, "grp", "row"), check_vma=False
    )
```

```python
import math

import jax
import jax.numpy as jnp
import numpy as np
from jax import lax
from jax.experimental import pallas as pl
from jax.experimental.pallas import tpu as pltpu
from jax.sharding import PartitionSpec as P

F = 16
KC = 128
SUB = 256
R_DEV = 32
SUB_DEV = 2
SUPPORT = 8
NOVER = 256
CHIP = 2 * R_DEV
LANES = 128
BLOCK = 1024
UNROLL = 4
PART = 512
PART_UNROLL = 8

TWO_PI = 2.0 * math.pi

VMEM = pl.BlockSpec(memory_space=pltpu.VMEM)
HBM = pl.BlockSpec(memory_space=pltpu.HBM)


def turned_rows():
    wave = np.arange(KC)
    place = wave // 8 * 16 + wave % 8
    return np.concatenate([place, place + 8])


def transform_table():
    kcol = np.arange(KC)
    jcol = np.arange(SUB)
    angles = np.float32(TWO_PI) * (kcol[:, None] * jcol[None, :] % SUB).astype(np.float32) / np.float32(SUB)
    scale = np.float32(1.0 / math.sqrt(KC))
    parts = np.concatenate([np.cos(angles) * scale, np.sin(angles) * scale], axis=0).astype(jnp.bfloat16)
    table = np.zeros_like(parts)
    table[turned_rows()] = parts
    return table


EXCHANGES = 4
LATER = 6


def reached(exchange, chip, chips):
    return (
        (chip + 2) % chips,
        (((chip + 1) ^ 1) + chips - 1) % chips,
        (chip + chips - 2) % chips,
        chip ^ 1,
    )[exchange]


def facet_products(factors, rows_ref, outs, half_step, first_row):
    for group in range(R_DEV // 16):
        rows = slice(16 * group, 16 * group + 16)
        cells = jnp.concatenate(
            [rows_ref[0, :, rows, :].reshape(F * 16, KC), rows_ref[1, :, rows, :].reshape(F * 16, KC)], axis=1
        )
        products = []
        for kind in range(2):
            high = jnp.dot(factors(group, 2 * kind), cells, preferred_element_type=jnp.float32)
            low = jnp.dot(factors(group, 2 * kind + 1), cells, preferred_element_type=jnp.float32)
            products.append(high + low)
        with_cos, with_sin = products
        real_part = (with_cos[:, :KC] - with_sin[:, KC:]).astype(jnp.bfloat16)
        imag_part = (with_cos[:, KC:] + with_sin[:, :KC]).astype(jnp.bfloat16)
        for place, out in enumerate(outs):
            for sub in range(SUB_DEV):
                here = slice((place * SUB_DEV + sub) * 16, (place * SUB_DEV + sub) * 16 + 16)
                first = first_row + sub * half_step + 16 * group
                if not isinstance(first, int):
                    first = pl.multiple_of(first, 16)
                out[pl.ds(first, 16), :KC] = real_part[here]
                out[pl.ds(first, 16), KC:] = imag_part[here]


def own_facet_kernel(
    devices,
    start_hbm,
    length_hbm,
    offset_hbm,
    window_hbm,
    rows_hbm,
    *rest,
):
    later_hbm, rest = rest[:LATER], rest[LATER:]
    outs, other_factors, shifts, later = rest[:5], rest[5], rest[6], rest[7 : 7 + LATER]
    start, length, offset, window, rows_ref, own_factors, padded, sems = rest[7 + LATER :]
    copies = [
        pltpu.make_async_copy(source, target, sems.at[number])
        for number, (source, target) in enumerate(
            (
                (start_hbm, start),
                (length_hbm, length),
                (offset_hbm, offset),
                (window_hbm, window),
                (rows_hbm, rows_ref),
                *zip(later_hbm, later),
            )
        )
    ]
    for copy in copies:
        copy.start()
    total_rows = devices * R_DEV
    chips = devices // 2
    position = lax.axis_index("row")
    chip = position // 2
    core = position % 2
    padded[:R_DEV, :] = jnp.zeros((R_DEV, F), jnp.float32)
    padded[R_DEV + SUB :, :] = jnp.zeros((R_DEV, F), jnp.float32)
    row_index = lax.broadcasted_iota(jnp.int32, (R_DEV, F), 0)
    lane = lax.broadcasted_iota(jnp.int32, (R_DEV, LANES), 1)
    sublane = lax.broadcasted_iota(jnp.int32, (R_DEV, LANES), 0)
    diagonal = (lane & 15) == (sublane & 15)

    def spread(values):
        wide = jnp.concatenate([values, jnp.zeros((R_DEV, LANES - F), values.dtype)], axis=1)
        return [
            jnp.concatenate(
                [
                    jnp.take_along_axis(
                        wide[row : row + 8], (lane[:8] >> 4) + 8 * side, axis=1, mode="promise_in_bounds"
                    )
                    for row in range(0, R_DEV, 8)
                ],
                axis=0,
            )
            for side in range(2)
        ]

    for copy in copies[:4]:
        copy.wait()
    padded[R_DEV : R_DEV + SUB, :] = jnp.transpose(window[...])
    for sub in range(SUB_DEV):
        shift = start[position * SUB_DEV + sub] - chip * CHIP
        shifts[sub] = jnp.full((8, LANES), shift, jnp.int32)
    for held, factors in enumerate((own_factors, other_factors)):
        half = core if held == 0 else 1 - core
        base = chip * CHIP + half * R_DEV
        turns = (offset[...] * (base + row_index)) & (total_rows - 1)
        angles = TWO_PI * turns.astype(jnp.float32) / total_rows
        phases = [
            [jnp.where(diagonal, side, 0.0) for side in spread(part)]
            for part in (jnp.cos(angles), jnp.sin(angles))
        ]
        for place in range(1 + EXCHANGES):
            target = chip if place == 0 else reached(place - 1, chip, chips)
            for sub in range(SUB_DEV):
                subgrid = (target * 2 + core) * SUB_DEV + sub
                slot = (base - start[subgrid]) & (total_rows - 1)
                slot = jnp.where(slot > total_rows - R_DEV, slot - total_rows, slot)
                slot = jnp.minimum(slot, SUB)
                piece = padded[pl.ds(slot + R_DEV, R_DEV), :]
                weights = spread(jnp.where(slot + row_index < length[subgrid], piece, 0.0))
                for kind in range(2):
                    for side in range(2):
                        exact = weights[side] * phases[kind][side]
                        high = exact.astype(jnp.bfloat16)
                        low = (exact - high.astype(jnp.float32)).astype(jnp.bfloat16)
                        lanes = slice(side * LANES, (side + 1) * LANES)
                        for group in range(R_DEV // 16):
                            rows = slice(16 * group, 16 * group + 16)
                            here = slice((place * SUB_DEV + sub) * 16, (place * SUB_DEV + sub) * 16 + 16)
                            factors[group, 2 * kind, here, lanes] = high[rows]
                            factors[group, 2 * kind + 1, here, lanes] = low[rows]
    copies[4].wait()
    facet_products(lambda group, kind: own_factors[group, kind], rows_ref, outs, R_DEV, 0)
    for copy in copies[5:]:
        copy.wait()


def other_facet_kernel(rows_ref, factors, shifts, *rest):
    earlier, outs, shifts_out = rest[:5], rest[5:10], rest[10]
    shifts_out[...] = shifts[...]
    core = lax.axis_index("row") % 2
    for piece, out in zip(earlier, outs):
        for sub in range(SUB_DEV):
            first = pl.multiple_of(sub * CHIP + core * R_DEV, R_DEV)
            out[pl.ds(first, R_DEV), :] = piece[sub * R_DEV : (sub + 1) * R_DEV, :]
    facet_products(lambda group, kind: factors[group, kind], rows_ref, outs, CHIP, (1 - core) * R_DEV)


def spread(low, high, cell, table_row):
    count = cell.shape[1]
    cell = jnp.broadcast_to(cell, (SUPPORT, count))
    table_row = jnp.broadcast_to(table_row, (SUPPORT, count))
    place = table_row & (LANES - 1)
    picked = []
    for first in range(0, count, LANES):
        index = place[:, first : first + LANES]
        from_low = jnp.take_along_axis(low, index, axis=1, mode="promise_in_bounds")
        from_high = jnp.take_along_axis(high, index, axis=1, mode="promise_in_bounds")
        picked.append(jnp.where(table_row[:, first : first + LANES] < LANES, from_low, from_high))
    weights = jnp.concatenate(picked, axis=1)
    for bit in range(3):
        turned = pltpu.roll(weights, 1 << bit, axis=0)
        weights = jnp.where((cell & (1 << bit)) != 0, turned, weights)
    sublane = lax.broadcasted_iota(jnp.int32, (SUPPORT, count), 0)
    tile = ((cell >> 3) + jnp.where(sublane < (cell & 7), 1, 0)) & (SUB // 8 - 1)
    odd = (tile & 1) != 0
    pair = (tile >> 1).astype(jnp.float32)
    pairs = jnp.concatenate([jnp.where(odd, -1.0, pair), jnp.where(odd, pair, -1.0)], axis=0).astype(jnp.bfloat16)
    both = jnp.concatenate([weights, weights], axis=0).astype(jnp.bfloat16)
    zero = jnp.zeros_like(both)
    return jnp.concatenate([jnp.where(pairs == jnp.bfloat16(t), both, zero) for t in range(SUB // 16)], axis=0)


def spread_kernel(
    shifts_ref,
    table_ref,
    transform_ref,
    row_ref,
    column_ref,
    row_kernel_ref,
    column_kernel_ref,
    row_spread,
    column_waves,
):
    low, high = table_ref[:, :LANES], table_ref[:, LANES:]

    def one_block(block, carry):
        lanes = pl.ds(pl.multiple_of(block * BLOCK, BLOCK), BLOCK)
        for sub in range(SUB_DEV):
            shift = jnp.concatenate([shifts_ref[sub, :1, :]] * (BLOCK // LANES), axis=1)
            cell_row = (row_ref[sub : sub + 1, lanes] + shift) & (SUB - 1)
            row_spread[sub, :, lanes] = spread(low, high, cell_row, row_kernel_ref[sub : sub + 1, lanes])
            columns = spread(low, high, column_ref[sub : sub + 1, lanes], column_kernel_ref[sub : sub + 1, lanes])
            column_waves[sub, :, lanes] = jnp.dot(transform_ref[...], columns, preferred_element_type=jnp.float32)
        return carry

    lax.fori_loop(0, row_ref.shape[1] // BLOCK, one_block, 0, unroll=UNROLL)


def degrid_kernel(
    per_dest,
    own_ref,
    far_below_ref,
    odd_edge_ref,
    far_above_ref,
    even_edge_ref,
    row_spread,
    column_waves,
    out_ref,
    waves,
    gathered,
):
    even = lax.axis_index("row") // 2 % 2 == 0
    wave = lax.broadcasted_iota(jnp.int32, (2 * KC, 2 * KC), 1)
    place = ((wave & (KC - 1)) >> 3) * 16 + (wave & 7) + jnp.where(wave < KC, 0, 8)
    turn = (lax.broadcasted_iota(jnp.int32, (2 * KC, 2 * KC), 0) == place).astype(jnp.float32).astype(jnp.bfloat16)
    for sub in range(SUB_DEV):
        rows = slice(sub * CHIP, sub * CHIP + CHIP)
        odd_edge, even_edge = odd_edge_ref[rows, :], even_edge_ref[rows, :]
        summed = jnp.concatenate(
            [
                own_ref[rows, :],
                jnp.where(even, even_edge, odd_edge),
                far_below_ref[rows, :] + far_above_ref[rows, :],
                jnp.where(even, odd_edge, even_edge),
            ],
            axis=0,
        )
        waves[sub] = lax.dot_general(
            turn, summed, (((1,), (1,)), ((), ())), preferred_element_type=jnp.float32
        ).astype(jnp.bfloat16)
    chunks = per_dest // LANES

    def one_block(block, carry):
        lanes = pl.ds(pl.multiple_of(block * PART, PART), PART)
        for sub in range(SUB_DEV):
            along = jnp.dot(waves[sub], row_spread[sub, :, lanes], preferred_element_type=jnp.float32)
            sums = [None, None]
            for t in range(KC // 8):
                real = slice(16 * t, 16 * t + 8)
                imag = slice(16 * t + 8, 16 * t + 16)
                real_wave = column_waves[sub, real, lanes]
                imag_wave = column_waves[sub, imag, lanes]
                terms = (
                    along[real] * real_wave - along[imag] * imag_wave,
                    along[real] * imag_wave + along[imag] * real_wave,
                )
                sums = [term if t == 0 else total + term for total, term in zip(sums, terms)]
            first = block * (PART // LANES * 4)
            for part in range(2):
                total = jnp.sum(sums[part], axis=0, keepdims=True)
                for place in range(PART // LANES):
                    row = place // chunks * 4 * chunks + (sub * 2 + part) * chunks + place % chunks
                    gathered[pl.ds(first + row, 1), :] = total[:, place * LANES : (place + 1) * LANES]
        return carry

    lax.fori_loop(0, row_spread.shape[2] // PART, one_block, 0, unroll=PART_UNROLL)
    out_ref[...] = gathered[...].astype(jnp.bfloat16)


def place_kernel(devices, chunks, in_ref, out_ref, wide):
    wide[...] = in_ref[...].astype(jnp.float32)
    for part in range(2):
        for chunk in range(chunks):
            out_ref[part, :, chunk * LANES : (chunk + 1) * LANES] = wide[
                pl.ds(part * chunks + chunk, devices * SUB_DEV, stride=2 * chunks), :
            ]


def local(
    facet_rows,
    range_start,
    range_length,
    facet_offset,
    window_table,
    kernel_table,
    cell_row,
    cell_column,
    kernel_row,
    kernel_column,
):
    devices = lax.axis_size("row")
    chips = devices // 2
    slots = cell_row.shape[1]
    per_dest = slots // devices
    chunks = per_dest // LANES
    other_rows = lax.ppermute(facet_rows, "row", [(i, i ^ 1) for i in range(devices)])
    small = pltpu.CompilerParams(vmem_limit_bytes=12 * 1024 * 1024)
    factors = jax.ShapeDtypeStruct((R_DEV // 16, 4, 5 * SUB_DEV * 16, 16 * F), jnp.bfloat16)
    later = (kernel_table.T, jnp.asarray(transform_table()), cell_row, cell_column, kernel_row, kernel_column)
    *own_pieces, other_factors, shifts, table, transform, rows, columns, row_kernels, column_kernels = pl.pallas_call(
        lambda *refs: own_facet_kernel(devices, *refs),
        out_shape=[jax.ShapeDtypeStruct((SUB_DEV * R_DEV, 2 * KC), jnp.bfloat16)] * 5
        + [factors, jax.ShapeDtypeStruct((SUB_DEV, 8, LANES), jnp.int32)]
        + [jax.ShapeDtypeStruct(value.shape, value.dtype) for value in later],
        in_specs=[HBM] * (5 + LATER),
        out_specs=[VMEM] * (7 + LATER),
        scratch_shapes=[
            pltpu.SMEM(range_start.shape, jnp.int32),
            pltpu.SMEM(range_length.shape, jnp.int32),
            pltpu.VMEM((1, F), jnp.int32),
            pltpu.VMEM(window_table.shape, jnp.float32),
            pltpu.VMEM(facet_rows.shape, jnp.bfloat16),
            pltpu.VMEM(factors.shape, jnp.bfloat16),
            pltpu.VMEM((SUB + 2 * R_DEV, F), jnp.float32),
            pltpu.SemaphoreType.DMA((5 + LATER,)),
        ],
        compiler_params=small,
        name="own_facet_sums",
    )(
        *(
            pltpu.with_memory_space_constraint(value, pltpu.HBM)
            for value in (range_start, range_length, facet_offset.reshape(1, F), window_table, facet_rows, *later)
        )
    )
    *pieces, shifts = pl.pallas_call(
        other_facet_kernel,
        out_shape=[jax.ShapeDtypeStruct((SUB_DEV * CHIP, 2 * KC), jnp.bfloat16)] * 5
        + [jax.ShapeDtypeStruct((SUB_DEV, 8, LANES), jnp.int32)],
        in_specs=[VMEM] * 8,
        out_specs=[VMEM] * 6,
        compiler_params=small,
        name="other_facet_sums",
    )(other_rows, other_factors, shifts, *own_pieces)
    came = []
    for exchange, piece in enumerate(pieces[1:]):
        pairs = [
            (2 * chip + core, 2 * reached(exchange, chip, chips) + core)
            for chip in range(chips)
            for core in range(2)
        ]
        came.append(lax.ppermute(piece, "row", pairs))
    rows_out = devices * 4 * chunks
    spread_shape = (SUB_DEV, SUB, slots)
    row_spread, column_waves = pl.pallas_call(
        spread_kernel,
        out_shape=[
            jax.ShapeDtypeStruct(spread_shape, jnp.bfloat16),
            jax.ShapeDtypeStruct(spread_shape, jnp.float32),
        ],
        in_specs=[VMEM] * 7,
        out_specs=[VMEM] * 2,
        compiler_params=small,
        cost_estimate=pl.CostEstimate(
            flops=2 * SUB_DEV * SUB * 2 * KC * slots, bytes_accessed=6 * SUB_DEV * SUB * slots, transcendentals=0
        ),
        name="spread",
    )(shifts, table, transform, rows, columns, row_kernels, column_kernels)
    results = pl.pallas_call(
        lambda *refs: degrid_kernel(per_dest, *refs),
        out_shape=jax.ShapeDtypeStruct((rows_out, LANES), jnp.bfloat16),
        in_specs=[VMEM] * 7,
        out_specs=VMEM,
        scratch_shapes=[
            pltpu.VMEM((SUB_DEV, 2 * KC, SUB), jnp.bfloat16),
            pltpu.VMEM((rows_out, LANES), jnp.float32),
        ],
        compiler_params=small,
        name="degrid",
    )(pieces[0], *came, row_spread, column_waves)
    received = lax.all_to_all(
        results.reshape(devices, 4 * chunks, LANES), "row", split_axis=0, concat_axis=0, tiled=True
    )
    return pl.pallas_call(
        lambda *refs: place_kernel(devices, chunks, *refs),
        out_shape=jax.ShapeDtypeStruct((2, devices * SUB_DEV, per_dest), jnp.float32),
        in_specs=[VMEM],
        out_specs=VMEM,
        scratch_shapes=[pltpu.VMEM((rows_out, LANES), jnp.float32)],
        compiler_params=small,
        name="place",
    )(received.reshape(rows_out, LANES))


def solution(mesh):
    placed = (
        P(None, None, ("grp", "row"), None),
        P("grp"),
        P("grp"),
        P("grp"),
        P(),
        P(),
        P(("grp", "row"), None),
        P(("grp", "row"), None),
        P(("grp", "row"), None),
        P(("grp", "row"), None),
    )
    return jax.shard_map(
        local, mesh=mesh, in_specs=placed, out_specs=P(None, "grp", "row"), check_vma=False
    )
```

```python
import math

import jax
import jax.numpy as jnp
import numpy as np
from jax import lax
from jax.experimental import pallas as pl
from jax.experimental.pallas import tpu as pltpu
from jax.sharding import PartitionSpec as P

F = 16
KC = 128
SUB = 256
R_DEV = 32
SUB_DEV = 2
SUPPORT = 8
NOVER = 256
CHIP = 2 * R_DEV
LANES = 128
BLOCK = 1024
UNROLL = 4
PART = 512
PART_UNROLL = 8

TWO_PI = 2.0 * math.pi

VMEM = pl.BlockSpec(memory_space=pltpu.VMEM)
HBM = pl.BlockSpec(memory_space=pltpu.HBM)


def turned_rows():
    wave = np.arange(KC)
    place = wave // 8 * 16 + wave % 8
    return np.concatenate([place, place + 8])


def transform_table():
    kcol = np.arange(KC)
    jcol = np.arange(SUB)
    angles = np.float32(TWO_PI) * (kcol[:, None] * jcol[None, :] % SUB).astype(np.float32) / np.float32(SUB)
    scale = np.float32(1.0 / math.sqrt(KC))
    parts = np.concatenate([np.cos(angles) * scale, np.sin(angles) * scale], axis=0).astype(jnp.bfloat16)
    table = np.zeros_like(parts)
    table[turned_rows()] = parts
    return table


EXCHANGES = 4
LATER = 6


def reached(exchange, chip, chips):
    return (
        (chip + 2) % chips,
        (((chip + 1) ^ 1) + chips - 1) % chips,
        (chip + chips - 2) % chips,
        chip ^ 1,
    )[exchange]


def facet_products(factors, rows_ref, outs, half_step, first_row):
    for group in range(R_DEV // 16):
        rows = slice(16 * group, 16 * group + 16)
        cells = jnp.concatenate(
            [rows_ref[0, :, rows, :].reshape(F * 16, KC), rows_ref[1, :, rows, :].reshape(F * 16, KC)], axis=1
        )
        products = []
        for kind in range(2):
            high = jnp.dot(factors(group, 2 * kind), cells, preferred_element_type=jnp.float32)
            low = jnp.dot(factors(group, 2 * kind + 1), cells, preferred_element_type=jnp.float32)
            products.append(high + low)
        with_cos, with_sin = products
        real_part = (with_cos[:, :KC] - with_sin[:, KC:]).astype(jnp.bfloat16)
        imag_part = (with_cos[:, KC:] + with_sin[:, :KC]).astype(jnp.bfloat16)
        for place, out in enumerate(outs):
            for sub in range(SUB_DEV):
                here = slice((place * SUB_DEV + sub) * 16, (place * SUB_DEV + sub) * 16 + 16)
                first = first_row + sub * half_step + 16 * group
                if not isinstance(first, int):
                    first = pl.multiple_of(first, 16)
                out[pl.ds(first, 16), :KC] = real_part[here]
                out[pl.ds(first, 16), KC:] = imag_part[here]


def own_facet_kernel(
    devices,
    start_hbm,
    length_hbm,
    offset_hbm,
    window_hbm,
    rows_hbm,
    *rest,
):
    later_hbm, rest = rest[:LATER], rest[LATER:]
    outs, other_factors, shifts, later = rest[:5], rest[5], rest[6], rest[7 : 7 + LATER]
    start, length, offset, window, rows_ref, own_factors, padded, sems = rest[7 + LATER :]
    copies = [
        pltpu.make_async_copy(source, target, sems.at[number])
        for number, (source, target) in enumerate(
            (
                (start_hbm, start),
                (length_hbm, length),
                (offset_hbm, offset),
                (window_hbm, window),
                (rows_hbm, rows_ref),
                *zip(later_hbm, later),
            )
        )
    ]
    for copy in copies:
        copy.start()
    total_rows = devices * R_DEV
    chips = devices // 2
    position = lax.axis_index("row")
    chip = position // 2
    core = position % 2
    padded[:R_DEV, :] = jnp.zeros((R_DEV, F), jnp.float32)
    padded[R_DEV + SUB :, :] = jnp.zeros((R_DEV, F), jnp.float32)
    row_index = lax.broadcasted_iota(jnp.int32, (R_DEV, F), 0)
    lane = lax.broadcasted_iota(jnp.int32, (R_DEV, LANES), 1)
    sublane = lax.broadcasted_iota(jnp.int32, (R_DEV, LANES), 0)
    diagonal = (lane & 15) == (sublane & 15)

    def spread(values):
        wide = jnp.concatenate([values, jnp.zeros((R_DEV, LANES - F), values.dtype)], axis=1)
        return [
            jnp.concatenate(
                [
                    jnp.take_along_axis(
                        wide[row : row + 8], (lane[:8] >> 4) + 8 * side, axis=1, mode="promise_in_bounds"
                    )
                    for row in range(0, R_DEV, 8)
                ],
                axis=0,
            )
            for side in range(2)
        ]

    for copy in copies[:4]:
        copy.wait()
    padded[R_DEV : R_DEV + SUB, :] = jnp.transpose(window[...])
    for sub in range(SUB_DEV):
        shift = start[position * SUB_DEV + sub] - chip * CHIP
        shifts[sub] = jnp.full((8, LANES), shift, jnp.int32)
    for held, factors in enumerate((own_factors, other_factors)):
        half = core if held == 0 else 1 - core
        base = chip * CHIP + half * R_DEV
        turns = (offset[...] * (base + row_index)) & (total_rows - 1)
        angles = TWO_PI * turns.astype(jnp.float32) / total_rows
        phases = [
            [jnp.where(diagonal, side, 0.0) for side in spread(part)]
            for part in (jnp.cos(angles), jnp.sin(angles))
        ]
        for place in range(1 + EXCHANGES):
            target = chip if place == 0 else reached(place - 1, chip, chips)
            for sub in range(SUB_DEV):
                subgrid = (target * 2 + (core if place == 0 else 1 - core)) * SUB_DEV + sub
                slot = (base - start[subgrid]) & (total_rows - 1)
                slot = jnp.where(slot > total_rows - R_DEV, slot - total_rows, slot)
                slot = jnp.minimum(slot, SUB)
                piece = padded[pl.ds(slot + R_DEV, R_DEV), :]
                weights = spread(jnp.where(slot + row_index < length[subgrid], piece, 0.0))
                for kind in range(2):
                    for side in range(2):
                        exact = weights[side] * phases[kind][side]
                        high = exact.astype(jnp.bfloat16)
                        low = (exact - high.astype(jnp.float32)).astype(jnp.bfloat16)
                        lanes = slice(side * LANES, (side + 1) * LANES)
                        for group in range(R_DEV // 16):
                            rows = slice(16 * group, 16 * group + 16)
                            here = slice((place * SUB_DEV + sub) * 16, (place * SUB_DEV + sub) * 16 + 16)
                            factors[group, 2 * kind, here, lanes] = high[rows]
                            factors[group, 2 * kind + 1, here, lanes] = low[rows]
    copies[4].wait()
    facet_products(lambda group, kind: own_factors[group, kind], rows_ref, outs, R_DEV, 0)
    for copy in copies[5:]:
        copy.wait()


def other_facet_kernel(rows_ref, factors, shifts, *rest):
    earlier, outs, shifts_out = rest[:5], rest[5:10], rest[10]
    shifts_out[...] = shifts[...]
    core = lax.axis_index("row") % 2
    for piece, out in zip(earlier, outs):
        for sub in range(SUB_DEV):
            first = pl.multiple_of(sub * CHIP + core * R_DEV, R_DEV)
            out[pl.ds(first, R_DEV), :] = piece[sub * R_DEV : (sub + 1) * R_DEV, :]
    facet_products(lambda group, kind: factors[group, kind], rows_ref, outs, CHIP, (1 - core) * R_DEV)


def spread(low, high, cell, table_row):
    count = cell.shape[1]
    cell = jnp.broadcast_to(cell, (SUPPORT, count))
    table_row = jnp.broadcast_to(table_row, (SUPPORT, count))
    place = table_row & (LANES - 1)
    picked = []
    for first in range(0, count, LANES):
        index = place[:, first : first + LANES]
        from_low = jnp.take_along_axis(low, index, axis=1, mode="promise_in_bounds")
        from_high = jnp.take_along_axis(high, index, axis=1, mode="promise_in_bounds")
        picked.append(jnp.where(table_row[:, first : first + LANES] < LANES, from_low, from_high))
    weights = jnp.concatenate(picked, axis=1)
    for bit in range(3):
        turned = pltpu.roll(weights, 1 << bit, axis=0)
        weights = jnp.where((cell & (1 << bit)) != 0, turned, weights)
    sublane = lax.broadcasted_iota(jnp.int32, (SUPPORT, count), 0)
    tile = ((cell >> 3) + jnp.where(sublane < (cell & 7), 1, 0)) & (SUB // 8 - 1)
    odd = (tile & 1) != 0
    pair = (tile >> 1).astype(jnp.float32)
    pairs = jnp.concatenate([jnp.where(odd, -1.0, pair), jnp.where(odd, pair, -1.0)], axis=0).astype(jnp.bfloat16)
    both = jnp.concatenate([weights, weights], axis=0).astype(jnp.bfloat16)
    zero = jnp.zeros_like(both)
    return jnp.concatenate([jnp.where(pairs == jnp.bfloat16(t), both, zero) for t in range(SUB // 16)], axis=0)


def spread_kernel(
    shifts_ref,
    table_ref,
    transform_ref,
    row_ref,
    column_ref,
    row_kernel_ref,
    column_kernel_ref,
    row_spread,
    column_waves,
):
    low, high = table_ref[:, :LANES], table_ref[:, LANES:]

    def one_block(block, carry):
        lanes = pl.ds(pl.multiple_of(block * BLOCK, BLOCK), BLOCK)
        for sub in range(SUB_DEV):
            shift = jnp.concatenate([shifts_ref[sub, :1, :]] * (BLOCK // LANES), axis=1)
            cell_row = (row_ref[sub : sub + 1, lanes] + shift) & (SUB - 1)
            row_spread[sub, :, lanes] = spread(low, high, cell_row, row_kernel_ref[sub : sub + 1, lanes])
            columns = spread(low, high, column_ref[sub : sub + 1, lanes], column_kernel_ref[sub : sub + 1, lanes])
            column_waves[sub, :, lanes] = jnp.dot(transform_ref[...], columns, preferred_element_type=jnp.float32)
        return carry

    lax.fori_loop(0, row_ref.shape[1] // BLOCK, one_block, 0, unroll=UNROLL)


def degrid_kernel(
    per_dest,
    own_ref,
    far_below_ref,
    odd_edge_ref,
    far_above_ref,
    even_edge_ref,
    row_spread,
    column_waves,
    out_ref,
    waves,
    gathered,
):
    even = lax.axis_index("row") // 2 % 2 == 0
    wave = lax.broadcasted_iota(jnp.int32, (2 * KC, 2 * KC), 1)
    place = ((wave & (KC - 1)) >> 3) * 16 + (wave & 7) + jnp.where(wave < KC, 0, 8)
    turn = (lax.broadcasted_iota(jnp.int32, (2 * KC, 2 * KC), 0) == place).astype(jnp.float32).astype(jnp.bfloat16)
    for sub in range(SUB_DEV):
        rows = slice(sub * CHIP, sub * CHIP + CHIP)
        odd_edge, even_edge = odd_edge_ref[rows, :], even_edge_ref[rows, :]
        summed = jnp.concatenate(
            [
                own_ref[rows, :],
                jnp.where(even, even_edge, odd_edge),
                far_below_ref[rows, :] + far_above_ref[rows, :],
                jnp.where(even, odd_edge, even_edge),
            ],
            axis=0,
        )
        waves[sub] = lax.dot_general(
            turn, summed, (((1,), (1,)), ((), ())), preferred_element_type=jnp.float32
        ).astype(jnp.bfloat16)
    chunks = per_dest // LANES

    def one_block(block, carry):
        lanes = pl.ds(pl.multiple_of(block * PART, PART), PART)
        for sub in range(SUB_DEV):
            along = jnp.dot(waves[sub], row_spread[sub, :, lanes], preferred_element_type=jnp.float32)
            sums = [None, None]
            for t in range(KC // 8):
                real = slice(16 * t, 16 * t + 8)
                imag = slice(16 * t + 8, 16 * t + 16)
                real_wave = column_waves[sub, real, lanes]
                imag_wave = column_waves[sub, imag, lanes]
                terms = (
                    along[real] * real_wave - along[imag] * imag_wave,
                    along[real] * imag_wave + along[imag] * real_wave,
                )
                sums = [term if t == 0 else total + term for total, term in zip(sums, terms)]
            first = block * (PART // LANES * 4)
            for part in range(2):
                total = jnp.sum(sums[part], axis=0, keepdims=True)
                for place in range(PART // LANES):
                    row = place // chunks * 4 * chunks + (sub * 2 + part) * chunks + place % chunks
                    gathered[pl.ds(first + row, 1), :] = total[:, place * LANES : (place + 1) * LANES]
        return carry

    lax.fori_loop(0, row_spread.shape[2] // PART, one_block, 0, unroll=PART_UNROLL)
    out_ref[...] = gathered[...].astype(jnp.bfloat16)


def place_kernel(devices, chunks, in_ref, out_ref, wide):
    wide[...] = in_ref[...].astype(jnp.float32)
    for part in range(2):
        for chunk in range(chunks):
            out_ref[part, :, chunk * LANES : (chunk + 1) * LANES] = wide[
                pl.ds(part * chunks + chunk, devices * SUB_DEV, stride=2 * chunks), :
            ]


def local(
    facet_rows,
    range_start,
    range_length,
    facet_offset,
    window_table,
    kernel_table,
    cell_row,
    cell_column,
    kernel_row,
    kernel_column,
):
    devices = lax.axis_size("row")
    chips = devices // 2
    slots = cell_row.shape[1]
    per_dest = slots // devices
    chunks = per_dest // LANES
    other_rows = lax.ppermute(facet_rows, "row", [(i, i ^ 1) for i in range(devices)])
    small = pltpu.CompilerParams(vmem_limit_bytes=12 * 1024 * 1024)
    factors = jax.ShapeDtypeStruct((R_DEV // 16, 4, 5 * SUB_DEV * 16, 16 * F), jnp.bfloat16)
    later = (kernel_table.T, jnp.asarray(transform_table()), cell_row, cell_column, kernel_row, kernel_column)
    *own_pieces, other_factors, shifts, table, transform, rows, columns, row_kernels, column_kernels = pl.pallas_call(
        lambda *refs: own_facet_kernel(devices, *refs),
        out_shape=[jax.ShapeDtypeStruct((SUB_DEV * R_DEV, 2 * KC), jnp.bfloat16)] * 5
        + [factors, jax.ShapeDtypeStruct((SUB_DEV, 8, LANES), jnp.int32)]
        + [jax.ShapeDtypeStruct(value.shape, value.dtype) for value in later],
        in_specs=[HBM] * (5 + LATER),
        out_specs=[VMEM] * (7 + LATER),
        scratch_shapes=[
            pltpu.SMEM(range_start.shape, jnp.int32),
            pltpu.SMEM(range_length.shape, jnp.int32),
            pltpu.VMEM((1, F), jnp.int32),
            pltpu.VMEM(window_table.shape, jnp.float32),
            pltpu.VMEM(facet_rows.shape, jnp.bfloat16),
            pltpu.VMEM(factors.shape, jnp.bfloat16),
            pltpu.VMEM((SUB + 2 * R_DEV, F), jnp.float32),
            pltpu.SemaphoreType.DMA((5 + LATER,)),
        ],
        compiler_params=small,
        name="own_facet_sums",
    )(
        *(
            pltpu.with_memory_space_constraint(value, pltpu.HBM)
            for value in (range_start, range_length, facet_offset.reshape(1, F), window_table, facet_rows, *later)
        )
    )
    *pieces, shifts = pl.pallas_call(
        other_facet_kernel,
        out_shape=[jax.ShapeDtypeStruct((SUB_DEV * CHIP, 2 * KC), jnp.bfloat16)] * 5
        + [jax.ShapeDtypeStruct((SUB_DEV, 8, LANES), jnp.int32)],
        in_specs=[VMEM] * 8,
        out_specs=[VMEM] * 6,
        compiler_params=small,
        name="other_facet_sums",
    )(other_rows, other_factors, shifts, *own_pieces)
    came = []
    for exchange, piece in enumerate(pieces[1:]):
        pairs = [
            (2 * chip + core, 2 * reached(exchange, chip, chips) + 1 - core)
            for chip in range(chips)
            for core in range(2)
        ]
        came.append(lax.ppermute(piece, "row", pairs))
    rows_out = devices * 4 * chunks
    spread_shape = (SUB_DEV, SUB, slots)
    row_spread, column_waves = pl.pallas_call(
        spread_kernel,
        out_shape=[
            jax.ShapeDtypeStruct(spread_shape, jnp.bfloat16),
            jax.ShapeDtypeStruct(spread_shape, jnp.float32),
        ],
        in_specs=[VMEM] * 7,
        out_specs=[VMEM] * 2,
        compiler_params=small,
        cost_estimate=pl.CostEstimate(
            flops=2 * SUB_DEV * SUB * 2 * KC * slots, bytes_accessed=6 * SUB_DEV * SUB * slots, transcendentals=0
        ),
        name="spread",
    )(shifts, table, transform, rows, columns, row_kernels, column_kernels)
    results = pl.pallas_call(
        lambda *refs: degrid_kernel(per_dest, *refs),
        out_shape=jax.ShapeDtypeStruct((rows_out, LANES), jnp.bfloat16),
        in_specs=[VMEM] * 7,
        out_specs=VMEM,
        scratch_shapes=[
            pltpu.VMEM((SUB_DEV, 2 * KC, SUB), jnp.bfloat16),
            pltpu.VMEM((rows_out, LANES), jnp.float32),
        ],
        compiler_params=small,
        name="degrid",
    )(pieces[0], *came, row_spread, column_waves)
    received = lax.all_to_all(
        results.reshape(devices, 4 * chunks, LANES), "row", split_axis=0, concat_axis=0, tiled=True
    )
    return pl.pallas_call(
        lambda *refs: place_kernel(devices, chunks, *refs),
        out_shape=jax.ShapeDtypeStruct((2, devices * SUB_DEV, per_dest), jnp.float32),
        in_specs=[VMEM],
        out_specs=VMEM,
        scratch_shapes=[pltpu.VMEM((rows_out, LANES), jnp.float32)],
        compiler_params=small,
        name="place",
    )(received.reshape(rows_out, LANES))


def solution(mesh):
    placed = (
        P(None, None, ("grp", "row"), None),
        P("grp"),
        P("grp"),
        P("grp"),
        P(),
        P(),
        P(("grp", "row"), None),
        P(("grp", "row"), None),
        P(("grp", "row"), None),
        P(("grp", "row"), None),
    )
    return jax.shard_map(
        local, mesh=mesh, in_specs=placed, out_specs=P(None, "grp", "row"), check_vma=False
    )
```

```python
import math

import jax
import jax.numpy as jnp
import numpy as np
from jax import lax
from jax.experimental import pallas as pl
from jax.experimental.pallas import tpu as pltpu
from jax.sharding import PartitionSpec as P

F = 16
KC = 128
SUB = 256
R_DEV = 32
SUB_DEV = 2
SUPPORT = 8
NOVER = 256
CHIP = 2 * R_DEV
LANES = 128
BLOCK = 1024
UNROLL = 8
PART = 512
PART_UNROLL = 16

TWO_PI = 2.0 * math.pi

VMEM = pl.BlockSpec(memory_space=pltpu.VMEM)
HBM = pl.BlockSpec(memory_space=pltpu.HBM)


def turned_rows():
    wave = np.arange(KC)
    place = wave // 8 * 16 + wave % 8
    return np.concatenate([place, place + 8])


def transform_table():
    kcol = np.arange(KC)
    jcol = np.arange(SUB)
    angles = np.float32(TWO_PI) * (kcol[:, None] * jcol[None, :] % SUB).astype(np.float32) / np.float32(SUB)
    scale = np.float32(1.0 / math.sqrt(KC))
    parts = np.concatenate([np.cos(angles) * scale, np.sin(angles) * scale], axis=0).astype(jnp.bfloat16)
    table = np.zeros_like(parts)
    table[turned_rows()] = parts
    return table


EXCHANGES = 4
LATER = 6


def reached(exchange, chip, chips):
    return (
        (chip + 2) % chips,
        (((chip + 1) ^ 1) + chips - 1) % chips,
        (chip + chips - 2) % chips,
        chip ^ 1,
    )[exchange]


def facet_products(factors, rows_ref, outs, half_step, first_row):
    for group in range(R_DEV // 16):
        rows = slice(16 * group, 16 * group + 16)
        cells = jnp.concatenate(
            [rows_ref[0, :, rows, :].reshape(F * 16, KC), rows_ref[1, :, rows, :].reshape(F * 16, KC)], axis=1
        )
        products = []
        for kind in range(2):
            high = jnp.dot(factors(group, 2 * kind), cells, preferred_element_type=jnp.float32)
            low = jnp.dot(factors(group, 2 * kind + 1), cells, preferred_element_type=jnp.float32)
            products.append(high + low)
        with_cos, with_sin = products
        real_part = (with_cos[:, :KC] - with_sin[:, KC:]).astype(jnp.bfloat16)
        imag_part = (with_cos[:, KC:] + with_sin[:, :KC]).astype(jnp.bfloat16)
        for place, out in enumerate(outs):
            for sub in range(SUB_DEV):
                here = slice((place * SUB_DEV + sub) * 16, (place * SUB_DEV + sub) * 16 + 16)
                first = first_row + sub * half_step + 16 * group
                if not isinstance(first, int):
                    first = pl.multiple_of(first, 16)
                out[pl.ds(first, 16), :KC] = real_part[here]
                out[pl.ds(first, 16), KC:] = imag_part[here]


def own_facet_kernel(
    devices,
    start_hbm,
    length_hbm,
    offset_hbm,
    window_hbm,
    rows_hbm,
    *rest,
):
    later_hbm, rest = rest[:LATER], rest[LATER:]
    outs, other_factors, shifts, later = rest[:5], rest[5], rest[6], rest[7 : 7 + LATER]
    start, length, offset, window, rows_ref, own_factors, padded, sems = rest[7 + LATER :]
    copies = [
        pltpu.make_async_copy(source, target, sems.at[number])
        for number, (source, target) in enumerate(
            (
                (start_hbm, start),
                (length_hbm, length),
                (offset_hbm, offset),
                (window_hbm, window),
                (rows_hbm, rows_ref),
                *zip(later_hbm, later),
            )
        )
    ]
    for copy in copies:
        copy.start()
    total_rows = devices * R_DEV
    chips = devices // 2
    position = lax.axis_index("row")
    chip = position // 2
    core = position % 2
    padded[:R_DEV, :] = jnp.zeros((R_DEV, F), jnp.float32)
    padded[R_DEV + SUB :, :] = jnp.zeros((R_DEV, F), jnp.float32)
    row_index = lax.broadcasted_iota(jnp.int32, (R_DEV, F), 0)
    lane = lax.broadcasted_iota(jnp.int32, (R_DEV, LANES), 1)
    sublane = lax.broadcasted_iota(jnp.int32, (R_DEV, LANES), 0)
    diagonal = (lane & 15) == (sublane & 15)

    def spread(values):
        wide = jnp.concatenate([values, jnp.zeros((R_DEV, LANES - F), values.dtype)], axis=1)
        return [
            jnp.concatenate(
                [
                    jnp.take_along_axis(
                        wide[row : row + 8], (lane[:8] >> 4) + 8 * side, axis=1, mode="promise_in_bounds"
                    )
                    for row in range(0, R_DEV, 8)
                ],
                axis=0,
            )
            for side in range(2)
        ]

    for copy in copies[:4]:
        copy.wait()
    padded[R_DEV : R_DEV + SUB, :] = jnp.transpose(window[...])
    for sub in range(SUB_DEV):
        shift = start[position * SUB_DEV + sub] - chip * CHIP
        shifts[sub] = jnp.full((8, LANES), shift, jnp.int32)
    for held, factors in enumerate((own_factors, other_factors)):
        half = core if held == 0 else 1 - core
        base = chip * CHIP + half * R_DEV
        turns = (offset[...] * (base + row_index)) & (total_rows - 1)
        angles = TWO_PI * turns.astype(jnp.float32) / total_rows
        phases = [
            [jnp.where(diagonal, side, 0.0) for side in spread(part)]
            for part in (jnp.cos(angles), jnp.sin(angles))
        ]
        for place in range(1 + EXCHANGES):
            target = chip if place == 0 else reached(place - 1, chip, chips)
            for sub in range(SUB_DEV):
                subgrid = (target * 2 + (core if place == 0 else 1 - core)) * SUB_DEV + sub
                slot = (base - start[subgrid]) & (total_rows - 1)
                slot = jnp.where(slot > total_rows - R_DEV, slot - total_rows, slot)
                slot = jnp.minimum(slot, SUB)
                piece = padded[pl.ds(slot + R_DEV, R_DEV), :]
                weights = spread(jnp.where(slot + row_index < length[subgrid], piece, 0.0))
                for kind in range(2):
                    for side in range(2):
                        exact = weights[side] * phases[kind][side]
                        high = exact.astype(jnp.bfloat16)
                        low = (exact - high.astype(jnp.float32)).astype(jnp.bfloat16)
                        lanes = slice(side * LANES, (side + 1) * LANES)
                        for group in range(R_DEV // 16):
                            rows = slice(16 * group, 16 * group + 16)
                            here = slice((place * SUB_DEV + sub) * 16, (place * SUB_DEV + sub) * 16 + 16)
                            factors[group, 2 * kind, here, lanes] = high[rows]
                            factors[group, 2 * kind + 1, here, lanes] = low[rows]
    copies[4].wait()
    facet_products(lambda group, kind: own_factors[group, kind], rows_ref, outs, R_DEV, 0)
    for copy in copies[5:]:
        copy.wait()


def other_facet_kernel(rows_ref, factors, shifts, *rest):
    earlier, outs, shifts_out = rest[:5], rest[5:10], rest[10]
    shifts_out[...] = shifts[...]
    core = lax.axis_index("row") % 2
    for piece, out in zip(earlier, outs):
        for sub in range(SUB_DEV):
            first = pl.multiple_of(sub * CHIP + core * R_DEV, R_DEV)
            out[pl.ds(first, R_DEV), :] = piece[sub * R_DEV : (sub + 1) * R_DEV, :]
    facet_products(lambda group, kind: factors[group, kind], rows_ref, outs, CHIP, (1 - core) * R_DEV)


def spread(low, high, cell, table_row):
    count = cell.shape[1]
    cell = jnp.broadcast_to(cell, (SUPPORT, count))
    table_row = jnp.broadcast_to(table_row, (SUPPORT, count))
    place = table_row & (LANES - 1)
    picked = []
    for first in range(0, count, LANES):
        index = place[:, first : first + LANES]
        from_low = jnp.take_along_axis(low, index, axis=1, mode="promise_in_bounds")
        from_high = jnp.take_along_axis(high, index, axis=1, mode="promise_in_bounds")
        picked.append(jnp.where(table_row[:, first : first + LANES] < LANES, from_low, from_high))
    weights = jnp.concatenate(picked, axis=1)
    for bit in range(3):
        turned = pltpu.roll(weights, 1 << bit, axis=0)
        weights = jnp.where((cell & (1 << bit)) != 0, turned, weights)
    sublane = lax.broadcasted_iota(jnp.int32, (SUPPORT, count), 0)
    tile = ((cell >> 3) + jnp.where(sublane < (cell & 7), 1, 0)) & (SUB // 8 - 1)
    odd = (tile & 1) != 0
    pair = (tile >> 1).astype(jnp.float32)
    pairs = jnp.concatenate([jnp.where(odd, -1.0, pair), jnp.where(odd, pair, -1.0)], axis=0).astype(jnp.bfloat16)
    both = jnp.concatenate([weights, weights], axis=0).astype(jnp.bfloat16)
    zero = jnp.zeros_like(both)
    return jnp.concatenate([jnp.where(pairs == jnp.bfloat16(t), both, zero) for t in range(SUB // 16)], axis=0)


def spread_kernel(
    shifts_ref,
    table_ref,
    transform_ref,
    row_ref,
    column_ref,
    row_kernel_ref,
    column_kernel_ref,
    row_spread,
    column_waves,
):
    low, high = table_ref[:, :LANES], table_ref[:, LANES:]

    def one_block(block, carry):
        lanes = pl.ds(pl.multiple_of(block * BLOCK, BLOCK), BLOCK)
        for sub in range(SUB_DEV):
            shift = jnp.concatenate([shifts_ref[sub, :1, :]] * (BLOCK // LANES), axis=1)
            cell_row = (row_ref[sub : sub + 1, lanes] + shift) & (SUB - 1)
            row_spread[sub, :, lanes] = spread(low, high, cell_row, row_kernel_ref[sub : sub + 1, lanes])
            columns = spread(low, high, column_ref[sub : sub + 1, lanes], column_kernel_ref[sub : sub + 1, lanes])
            column_waves[sub, :, lanes] = jnp.dot(transform_ref[...], columns, preferred_element_type=jnp.float32)
        return carry

    lax.fori_loop(0, row_ref.shape[1] // BLOCK, one_block, 0, unroll=UNROLL)


def degrid_kernel(
    per_dest,
    own_ref,
    far_below_ref,
    odd_edge_ref,
    far_above_ref,
    even_edge_ref,
    row_spread,
    column_waves,
    out_ref,
    waves,
    gathered,
):
    even = lax.axis_index("row") // 2 % 2 == 0
    wave = lax.broadcasted_iota(jnp.int32, (2 * KC, 2 * KC), 1)
    place = ((wave & (KC - 1)) >> 3) * 16 + (wave & 7) + jnp.where(wave < KC, 0, 8)
    turn = (lax.broadcasted_iota(jnp.int32, (2 * KC, 2 * KC), 0) == place).astype(jnp.float32).astype(jnp.bfloat16)
    for sub in range(SUB_DEV):
        rows = slice(sub * CHIP, sub * CHIP + CHIP)
        odd_edge, even_edge = odd_edge_ref[rows, :], even_edge_ref[rows, :]
        summed = jnp.concatenate(
            [
                own_ref[rows, :],
                jnp.where(even, even_edge, odd_edge),
                far_below_ref[rows, :] + far_above_ref[rows, :],
                jnp.where(even, odd_edge, even_edge),
            ],
            axis=0,
        )
        waves[sub] = lax.dot_general(
            turn, summed, (((1,), (1,)), ((), ())), preferred_element_type=jnp.float32
        ).astype(jnp.bfloat16)
    chunks = per_dest // LANES

    def one_block(block, carry):
        lanes = pl.ds(pl.multiple_of(block * PART, PART), PART)
        for sub in range(SUB_DEV):
            along = jnp.dot(waves[sub], row_spread[sub, :, lanes], preferred_element_type=jnp.float32)
            sums = [None, None]
            for t in range(KC // 8):
                real = slice(16 * t, 16 * t + 8)
                imag = slice(16 * t + 8, 16 * t + 16)
                real_wave = column_waves[sub, real, lanes]
                imag_wave = column_waves[sub, imag, lanes]
                terms = (
                    along[real] * real_wave - along[imag] * imag_wave,
                    along[real] * imag_wave + along[imag] * real_wave,
                )
                sums = [term if t == 0 else total + term for total, term in zip(sums, terms)]
            first = block * (PART // LANES * 4)
            for part in range(2):
                total = jnp.sum(sums[part], axis=0, keepdims=True)
                for place in range(PART // LANES):
                    row = place // chunks * 4 * chunks + (sub * 2 + part) * chunks + place % chunks
                    gathered[pl.ds(first + row, 1), :] = total[:, place * LANES : (place + 1) * LANES]
        return carry

    lax.fori_loop(0, row_spread.shape[2] // PART, one_block, 0, unroll=PART_UNROLL)
    out_ref[...] = gathered[...].astype(jnp.bfloat16)


def place_kernel(devices, chunks, in_ref, out_ref, wide):
    wide[...] = in_ref[...].astype(jnp.float32)
    for part in range(2):
        for chunk in range(chunks):
            out_ref[part, :, chunk * LANES : (chunk + 1) * LANES] = wide[
                pl.ds(part * chunks + chunk, devices * SUB_DEV, stride=2 * chunks), :
            ]


def local(
    facet_rows,
    range_start,
    range_length,
    facet_offset,
    window_table,
    kernel_table,
    cell_row,
    cell_column,
    kernel_row,
    kernel_column,
):
    devices = lax.axis_size("row")
    chips = devices // 2
    slots = cell_row.shape[1]
    per_dest = slots // devices
    chunks = per_dest // LANES
    other_rows = lax.ppermute(facet_rows, "row", [(i, i ^ 1) for i in range(devices)])
    small = pltpu.CompilerParams(vmem_limit_bytes=12 * 1024 * 1024)
    factors = jax.ShapeDtypeStruct((R_DEV // 16, 4, 5 * SUB_DEV * 16, 16 * F), jnp.bfloat16)
    later = (kernel_table.T, jnp.asarray(transform_table()), cell_row, cell_column, kernel_row, kernel_column)
    *own_pieces, other_factors, shifts, table, transform, rows, columns, row_kernels, column_kernels = pl.pallas_call(
        lambda *refs: own_facet_kernel(devices, *refs),
        out_shape=[jax.ShapeDtypeStruct((SUB_DEV * R_DEV, 2 * KC), jnp.bfloat16)] * 5
        + [factors, jax.ShapeDtypeStruct((SUB_DEV, 8, LANES), jnp.int32)]
        + [jax.ShapeDtypeStruct(value.shape, value.dtype) for value in later],
        in_specs=[HBM] * (5 + LATER),
        out_specs=[VMEM] * (7 + LATER),
        scratch_shapes=[
            pltpu.SMEM(range_start.shape, jnp.int32),
            pltpu.SMEM(range_length.shape, jnp.int32),
            pltpu.VMEM((1, F), jnp.int32),
            pltpu.VMEM(window_table.shape, jnp.float32),
            pltpu.VMEM(facet_rows.shape, jnp.bfloat16),
            pltpu.VMEM(factors.shape, jnp.bfloat16),
            pltpu.VMEM((SUB + 2 * R_DEV, F), jnp.float32),
            pltpu.SemaphoreType.DMA((5 + LATER,)),
        ],
        compiler_params=small,
        name="own_facet_sums",
    )(
        *(
            pltpu.with_memory_space_constraint(value, pltpu.HBM)
            for value in (range_start, range_length, facet_offset.reshape(1, F), window_table, facet_rows, *later)
        )
    )
    *pieces, shifts = pl.pallas_call(
        other_facet_kernel,
        out_shape=[jax.ShapeDtypeStruct((SUB_DEV * CHIP, 2 * KC), jnp.bfloat16)] * 5
        + [jax.ShapeDtypeStruct((SUB_DEV, 8, LANES), jnp.int32)],
        in_specs=[VMEM] * 8,
        out_specs=[VMEM] * 6,
        compiler_params=small,
        name="other_facet_sums",
    )(other_rows, other_factors, shifts, *own_pieces)
    came = []
    for exchange, piece in enumerate(pieces[1:]):
        pairs = [
            (2 * chip + core, 2 * reached(exchange, chip, chips) + 1 - core)
            for chip in range(chips)
            for core in range(2)
        ]
        came.append(lax.ppermute(piece, "row", pairs))
    rows_out = devices * 4 * chunks
    spread_shape = (SUB_DEV, SUB, slots)
    row_spread, column_waves = pl.pallas_call(
        spread_kernel,
        out_shape=[
            jax.ShapeDtypeStruct(spread_shape, jnp.bfloat16),
            jax.ShapeDtypeStruct(spread_shape, jnp.float32),
        ],
        in_specs=[VMEM] * 7,
        out_specs=[VMEM] * 2,
        compiler_params=small,
        cost_estimate=pl.CostEstimate(
            flops=2 * SUB_DEV * SUB * 2 * KC * slots, bytes_accessed=6 * SUB_DEV * SUB * slots, transcendentals=0
        ),
        name="spread",
    )(shifts, table, transform, rows, columns, row_kernels, column_kernels)
    results = pl.pallas_call(
        lambda *refs: degrid_kernel(per_dest, *refs),
        out_shape=jax.ShapeDtypeStruct((rows_out, LANES), jnp.bfloat16),
        in_specs=[VMEM] * 7,
        out_specs=VMEM,
        scratch_shapes=[
            pltpu.VMEM((SUB_DEV, 2 * KC, SUB), jnp.bfloat16),
            pltpu.VMEM((rows_out, LANES), jnp.float32),
        ],
        compiler_params=small,
        name="degrid",
    )(pieces[0], *came, row_spread, column_waves)
    received = lax.all_to_all(
        results.reshape(devices, 4 * chunks, LANES), "row", split_axis=0, concat_axis=0, tiled=True
    )
    return pl.pallas_call(
        lambda *refs: place_kernel(devices, chunks, *refs),
        out_shape=jax.ShapeDtypeStruct((2, devices * SUB_DEV, per_dest), jnp.float32),
        in_specs=[VMEM],
        out_specs=VMEM,
        scratch_shapes=[pltpu.VMEM((rows_out, LANES), jnp.float32)],
        compiler_params=small,
        name="place",
    )(received.reshape(rows_out, LANES))


def solution(mesh):
    placed = (
        P(None, None, ("grp", "row"), None),
        P("grp"),
        P("grp"),
        P("grp"),
        P(),
        P(),
        P(("grp", "row"), None),
        P(("grp", "row"), None),
        P(("grp", "row"), None),
        P(("grp", "row"), None),
    )
    return jax.shard_map(
        local, mesh=mesh, in_specs=placed, out_specs=P(None, "grp", "row"), check_vma=False
    )
```

```python
import math

import jax
import jax.numpy as jnp
import numpy as np
from jax import lax
from jax.experimental import pallas as pl
from jax.experimental.pallas import tpu as pltpu
from jax.sharding import PartitionSpec as P

F = 16
KC = 128
SUB = 256
R_DEV = 32
SUB_DEV = 2
SUPPORT = 8
NOVER = 256
CHIP = 2 * R_DEV
LANES = 128
BLOCK = 1024
UNROLL = 8
PART = 512
PART_UNROLL = 16

TWO_PI = 2.0 * math.pi

VMEM = pl.BlockSpec(memory_space=pltpu.VMEM)
HBM = pl.BlockSpec(memory_space=pltpu.HBM)


def turned_rows():
    wave = np.arange(KC)
    place = wave // 8 * 16 + wave % 8
    return np.concatenate([place, place + 8])


def transform_table():
    kcol = np.arange(KC)
    jcol = np.arange(SUB)
    angles = np.float32(TWO_PI) * (kcol[:, None] * jcol[None, :] % SUB).astype(np.float32) / np.float32(SUB)
    scale = np.float32(1.0 / math.sqrt(KC))
    parts = np.concatenate([np.cos(angles) * scale, np.sin(angles) * scale], axis=0).astype(jnp.bfloat16)
    table = np.zeros_like(parts)
    table[turned_rows()] = parts
    return table


EXCHANGES = 4
LATER = 6


def reached(exchange, chip, chips):
    return (
        (chip + 2) % chips,
        (((chip + 1) ^ 1) + chips - 1) % chips,
        (chip + chips - 2) % chips,
        chip ^ 1,
    )[exchange]


def facet_products(factors, rows_ref, outs, half_step, first_row):
    for group in range(R_DEV // 16):
        rows = slice(16 * group, 16 * group + 16)
        cells = jnp.concatenate(
            [rows_ref[0, :, rows, :].reshape(F * 16, KC), rows_ref[1, :, rows, :].reshape(F * 16, KC)], axis=1
        )
        products = []
        for kind in range(2):
            high = jnp.dot(factors(group, 2 * kind), cells, preferred_element_type=jnp.float32)
            low = jnp.dot(factors(group, 2 * kind + 1), cells, preferred_element_type=jnp.float32)
            products.append(high + low)
        with_cos, with_sin = products
        real_part = (with_cos[:, :KC] - with_sin[:, KC:]).astype(jnp.bfloat16)
        imag_part = (with_cos[:, KC:] + with_sin[:, :KC]).astype(jnp.bfloat16)
        for place, out in enumerate(outs):
            for sub in range(SUB_DEV):
                here = slice((place * SUB_DEV + sub) * 16, (place * SUB_DEV + sub) * 16 + 16)
                first = first_row + sub * half_step + 16 * group
                if not isinstance(first, int):
                    first = pl.multiple_of(first, 16)
                out[pl.ds(first, 16), :KC] = real_part[here]
                out[pl.ds(first, 16), KC:] = imag_part[here]


def own_facet_kernel(
    devices,
    start_hbm,
    length_hbm,
    offset_hbm,
    window_hbm,
    rows_hbm,
    *rest,
):
    later_hbm, rest = rest[:LATER], rest[LATER:]
    outs, other_factors, shifts, later = rest[:5], rest[5], rest[6], rest[7 : 7 + LATER]
    start, length, offset, window, rows_ref, own_factors, padded, sems = rest[7 + LATER :]
    copies = [
        pltpu.make_async_copy(source, target, sems.at[number])
        for number, (source, target) in enumerate(
            (
                (start_hbm, start),
                (length_hbm, length),
                (offset_hbm, offset),
                (window_hbm, window),
                (rows_hbm, rows_ref),
                *zip(later_hbm, later),
            )
        )
    ]
    for copy in copies:
        copy.start()
    total_rows = devices * R_DEV
    chips = devices // 2
    position = lax.axis_index("row")
    chip = position // 2
    core = position % 2
    padded[:R_DEV, :] = jnp.zeros((R_DEV, F), jnp.float32)
    padded[R_DEV + SUB :, :] = jnp.zeros((R_DEV, F), jnp.float32)
    row_index = lax.broadcasted_iota(jnp.int32, (R_DEV, F), 0)
    lane = lax.broadcasted_iota(jnp.int32, (R_DEV, LANES), 1)
    sublane = lax.broadcasted_iota(jnp.int32, (R_DEV, LANES), 0)
    diagonal = (lane & 15) == (sublane & 15)

    def spread(values):
        wide = jnp.concatenate([values, jnp.zeros((R_DEV, LANES - F), values.dtype)], axis=1)
        return [
            jnp.concatenate(
                [
                    jnp.take_along_axis(
                        wide[row : row + 8], (lane[:8] >> 4) + 8 * side, axis=1, mode="promise_in_bounds"
                    )
                    for row in range(0, R_DEV, 8)
                ],
                axis=0,
            )
            for side in range(2)
        ]

    for copy in copies[:4]:
        copy.wait()
    padded[R_DEV : R_DEV + SUB, :] = jnp.transpose(window[...])
    for sub in range(SUB_DEV):
        shift = start[position * SUB_DEV + sub] - chip * CHIP
        shifts[sub] = jnp.full((8, LANES), shift, jnp.int32)
    for held, factors in enumerate((own_factors, other_factors)):
        half = core if held == 0 else 1 - core
        base = chip * CHIP + half * R_DEV
        turns = (offset[...] * (base + row_index)) & (total_rows - 1)
        angles = TWO_PI * turns.astype(jnp.float32) / total_rows
        phases = [
            [jnp.where(diagonal, side, 0.0) for side in spread(part)]
            for part in (jnp.cos(angles), jnp.sin(angles))
        ]
        for place in range(1 + EXCHANGES):
            target = chip if place == 0 else reached(place - 1, chip, chips)
            for sub in range(SUB_DEV):
                subgrid = (target * 2 + (core if place == 0 else 1 - core)) * SUB_DEV + sub
                slot = (base - start[subgrid]) & (total_rows - 1)
                slot = jnp.where(slot > total_rows - R_DEV, slot - total_rows, slot)
                slot = jnp.minimum(slot, SUB)
                piece = padded[pl.ds(slot + R_DEV, R_DEV), :]
                weights = spread(jnp.where(slot + row_index < length[subgrid], piece, 0.0))
                for kind in range(2):
                    for side in range(2):
                        exact = weights[side] * phases[kind][side]
                        high = exact.astype(jnp.bfloat16)
                        low = (exact - high.astype(jnp.float32)).astype(jnp.bfloat16)
                        lanes = slice(side * LANES, (side + 1) * LANES)
                        for group in range(R_DEV // 16):
                            rows = slice(16 * group, 16 * group + 16)
                            here = slice((place * SUB_DEV + sub) * 16, (place * SUB_DEV + sub) * 16 + 16)
                            factors[group, 2 * kind, here, lanes] = high[rows]
                            factors[group, 2 * kind + 1, here, lanes] = low[rows]
        if held == 0:
            copies[4].wait()
            facet_products(lambda group, kind: own_factors[group, kind], rows_ref, outs, R_DEV, 0)
    for copy in copies[5:]:
        copy.wait()


def other_facet_kernel(rows_ref, factors, shifts, *rest):
    earlier, outs, shifts_out = rest[:5], rest[5:10], rest[10]
    shifts_out[...] = shifts[...]
    core = lax.axis_index("row") % 2
    for piece, out in zip(earlier, outs):
        for sub in range(SUB_DEV):
            first = pl.multiple_of(sub * CHIP + core * R_DEV, R_DEV)
            out[pl.ds(first, R_DEV), :] = piece[sub * R_DEV : (sub + 1) * R_DEV, :]
    facet_products(lambda group, kind: factors[group, kind], rows_ref, outs, CHIP, (1 - core) * R_DEV)


def spread(low, high, cell, table_row):
    count = cell.shape[1]
    cell = jnp.broadcast_to(cell, (SUPPORT, count))
    table_row = jnp.broadcast_to(table_row, (SUPPORT, count))
    place = table_row & (LANES - 1)
    picked = []
    for first in range(0, count, LANES):
        index = place[:, first : first + LANES]
        from_low = jnp.take_along_axis(low, index, axis=1, mode="promise_in_bounds")
        from_high = jnp.take_along_axis(high, index, axis=1, mode="promise_in_bounds")
        picked.append(jnp.where(table_row[:, first : first + LANES] < LANES, from_low, from_high))
    weights = jnp.concatenate(picked, axis=1)
    for bit in range(3):
        turned = pltpu.roll(weights, 1 << bit, axis=0)
        weights = jnp.where((cell & (1 << bit)) != 0, turned, weights)
    sublane = lax.broadcasted_iota(jnp.int32, (SUPPORT, count), 0)
    tile = ((cell >> 3) + jnp.where(sublane < (cell & 7), 1, 0)) & (SUB // 8 - 1)
    odd = (tile & 1) != 0
    pair = (tile >> 1).astype(jnp.float32)
    pairs = jnp.concatenate([jnp.where(odd, -1.0, pair), jnp.where(odd, pair, -1.0)], axis=0).astype(jnp.bfloat16)
    both = jnp.concatenate([weights, weights], axis=0).astype(jnp.bfloat16)
    zero = jnp.zeros_like(both)
    return jnp.concatenate([jnp.where(pairs == jnp.bfloat16(t), both, zero) for t in range(SUB // 16)], axis=0)


def spread_kernel(
    shifts_ref,
    table_ref,
    transform_ref,
    row_ref,
    column_ref,
    row_kernel_ref,
    column_kernel_ref,
    row_spread,
    column_waves,
):
    low, high = table_ref[:, :LANES], table_ref[:, LANES:]

    def one_block(block, carry):
        lanes = pl.ds(pl.multiple_of(block * BLOCK, BLOCK), BLOCK)
        for sub in range(SUB_DEV):
            shift = jnp.concatenate([shifts_ref[sub, :1, :]] * (BLOCK // LANES), axis=1)
            cell_row = (row_ref[sub : sub + 1, lanes] + shift) & (SUB - 1)
            row_spread[sub, :, lanes] = spread(low, high, cell_row, row_kernel_ref[sub : sub + 1, lanes])
            columns = spread(low, high, column_ref[sub : sub + 1, lanes], column_kernel_ref[sub : sub + 1, lanes])
            column_waves[sub, :, lanes] = jnp.dot(transform_ref[...], columns, preferred_element_type=jnp.float32)
        return carry

    lax.fori_loop(0, row_ref.shape[1] // BLOCK, one_block, 0, unroll=UNROLL)


def degrid_kernel(
    per_dest,
    own_ref,
    far_below_ref,
    odd_edge_ref,
    far_above_ref,
    even_edge_ref,
    row_spread,
    column_waves,
    out_ref,
    waves,
    gathered,
):
    even = lax.axis_index("row") // 2 % 2 == 0
    wave = lax.broadcasted_iota(jnp.int32, (2 * KC, 2 * KC), 1)
    place = ((wave & (KC - 1)) >> 3) * 16 + (wave & 7) + jnp.where(wave < KC, 0, 8)
    turn = (lax.broadcasted_iota(jnp.int32, (2 * KC, 2 * KC), 0) == place).astype(jnp.float32).astype(jnp.bfloat16)
    for sub in range(SUB_DEV):
        rows = slice(sub * CHIP, sub * CHIP + CHIP)
        odd_edge, even_edge = odd_edge_ref[rows, :], even_edge_ref[rows, :]
        summed = jnp.concatenate(
            [
                own_ref[rows, :],
                jnp.where(even, even_edge, odd_edge),
                far_below_ref[rows, :] + far_above_ref[rows, :],
                jnp.where(even, odd_edge, even_edge),
            ],
            axis=0,
        )
        waves[sub] = lax.dot_general(
            turn, summed, (((1,), (1,)), ((), ())), preferred_element_type=jnp.float32
        ).astype(jnp.bfloat16)
    chunks = per_dest // LANES

    def one_block(block, carry):
        lanes = pl.ds(pl.multiple_of(block * PART, PART), PART)
        for sub in range(SUB_DEV):
            along = jnp.dot(waves[sub], row_spread[sub, :, lanes], preferred_element_type=jnp.float32)
            sums = [None, None]
            for t in range(KC // 8):
                real = slice(16 * t, 16 * t + 8)
                imag = slice(16 * t + 8, 16 * t + 16)
                real_wave = column_waves[sub, real, lanes]
                imag_wave = column_waves[sub, imag, lanes]
                terms = (
                    along[real] * real_wave - along[imag] * imag_wave,
                    along[real] * imag_wave + along[imag] * real_wave,
                )
                sums = [term if t == 0 else total + term for total, term in zip(sums, terms)]
            first = block * (PART // LANES * 4)
            for part in range(2):
                total = jnp.sum(sums[part], axis=0, keepdims=True)
                for place in range(PART // LANES):
                    row = place // chunks * 4 * chunks + (sub * 2 + part) * chunks + place % chunks
                    gathered[pl.ds(first + row, 1), :] = total[:, place * LANES : (place + 1) * LANES]
        return carry

    lax.fori_loop(0, row_spread.shape[2] // PART, one_block, 0, unroll=PART_UNROLL)
    out_ref[...] = gathered[...].astype(jnp.bfloat16)


def place_kernel(devices, chunks, in_ref, out_ref, wide):
    wide[...] = in_ref[...].astype(jnp.float32)
    for part in range(2):
        for chunk in range(chunks):
            out_ref[part, :, chunk * LANES : (chunk + 1) * LANES] = wide[
                pl.ds(part * chunks + chunk, devices * SUB_DEV, stride=2 * chunks), :
            ]


def local(
    facet_rows,
    range_start,
    range_length,
    facet_offset,
    window_table,
    kernel_table,
    cell_row,
    cell_column,
    kernel_row,
    kernel_column,
):
    devices = lax.axis_size("row")
    chips = devices // 2
    slots = cell_row.shape[1]
    per_dest = slots // devices
    chunks = per_dest // LANES
    other_rows = lax.ppermute(facet_rows, "row", [(i, i ^ 1) for i in range(devices)])
    small = pltpu.CompilerParams(vmem_limit_bytes=12 * 1024 * 1024)
    factors = jax.ShapeDtypeStruct((R_DEV // 16, 4, 5 * SUB_DEV * 16, 16 * F), jnp.bfloat16)
    later = (kernel_table.T, jnp.asarray(transform_table()), cell_row, cell_column, kernel_row, kernel_column)
    *own_pieces, other_factors, shifts, table, transform, rows, columns, row_kernels, column_kernels = pl.pallas_call(
        lambda *refs: own_facet_kernel(devices, *refs),
        out_shape=[jax.ShapeDtypeStruct((SUB_DEV * R_DEV, 2 * KC), jnp.bfloat16)] * 5
        + [factors, jax.ShapeDtypeStruct((SUB_DEV, 8, LANES), jnp.int32)]
        + [jax.ShapeDtypeStruct(value.shape, value.dtype) for value in later],
        in_specs=[HBM] * (5 + LATER),
        out_specs=[VMEM] * (7 + LATER),
        scratch_shapes=[
            pltpu.SMEM(range_start.shape, jnp.int32),
            pltpu.SMEM(range_length.shape, jnp.int32),
            pltpu.VMEM((1, F), jnp.int32),
            pltpu.VMEM(window_table.shape, jnp.float32),
            pltpu.VMEM(facet_rows.shape, jnp.bfloat16),
            pltpu.VMEM(factors.shape, jnp.bfloat16),
            pltpu.VMEM((SUB + 2 * R_DEV, F), jnp.float32),
            pltpu.SemaphoreType.DMA((5 + LATER,)),
        ],
        compiler_params=small,
        name="own_facet_sums",
    )(
        *(
            pltpu.with_memory_space_constraint(value, pltpu.HBM)
            for value in (range_start, range_length, facet_offset.reshape(1, F), window_table, facet_rows, *later)
        )
    )
    *pieces, shifts = pl.pallas_call(
        other_facet_kernel,
        out_shape=[jax.ShapeDtypeStruct((SUB_DEV * CHIP, 2 * KC), jnp.bfloat16)] * 5
        + [jax.ShapeDtypeStruct((SUB_DEV, 8, LANES), jnp.int32)],
        in_specs=[VMEM] * 8,
        out_specs=[VMEM] * 6,
        compiler_params=small,
        name="other_facet_sums",
    )(other_rows, other_factors, shifts, *own_pieces)
    came = []
    for exchange, piece in enumerate(pieces[1:]):
        pairs = [
            (2 * chip + core, 2 * reached(exchange, chip, chips) + 1 - core)
            for chip in range(chips)
            for core in range(2)
        ]
        came.append(lax.ppermute(piece, "row", pairs))
    rows_out = devices * 4 * chunks
    spread_shape = (SUB_DEV, SUB, slots)
    row_spread, column_waves = pl.pallas_call(
        spread_kernel,
        out_shape=[
            jax.ShapeDtypeStruct(spread_shape, jnp.bfloat16),
            jax.ShapeDtypeStruct(spread_shape, jnp.float32),
        ],
        in_specs=[VMEM] * 7,
        out_specs=[VMEM] * 2,
        compiler_params=small,
        cost_estimate=pl.CostEstimate(
            flops=2 * SUB_DEV * SUB * 2 * KC * slots, bytes_accessed=6 * SUB_DEV * SUB * slots, transcendentals=0
        ),
        name="spread",
    )(shifts, table, transform, rows, columns, row_kernels, column_kernels)
    results = pl.pallas_call(
        lambda *refs: degrid_kernel(per_dest, *refs),
        out_shape=jax.ShapeDtypeStruct((rows_out, LANES), jnp.bfloat16),
        in_specs=[VMEM] * 7,
        out_specs=VMEM,
        scratch_shapes=[
            pltpu.VMEM((SUB_DEV, 2 * KC, SUB), jnp.bfloat16),
            pltpu.VMEM((rows_out, LANES), jnp.float32),
        ],
        compiler_params=small,
        name="degrid",
    )(pieces[0], *came, row_spread, column_waves)
    received = lax.all_to_all(
        results.reshape(devices, 4 * chunks, LANES), "row", split_axis=0, concat_axis=0, tiled=True
    )
    return pl.pallas_call(
        lambda *refs: place_kernel(devices, chunks, *refs),
        out_shape=jax.ShapeDtypeStruct((2, devices * SUB_DEV, per_dest), jnp.float32),
        in_specs=[VMEM],
        out_specs=VMEM,
        scratch_shapes=[pltpu.VMEM((rows_out, LANES), jnp.float32)],
        compiler_params=small,
        name="place",
    )(received.reshape(rows_out, LANES))


def solution(mesh):
    placed = (
        P(None, None, ("grp", "row"), None),
        P("grp"),
        P("grp"),
        P("grp"),
        P(),
        P(),
        P(("grp", "row"), None),
        P(("grp", "row"), None),
        P(("grp", "row"), None),
        P(("grp", "row"), None),
    )
    return jax.shard_map(
        local, mesh=mesh, in_specs=placed, out_specs=P(None, "grp", "row"), check_vma=False
    )
```

```python
import math

import jax
import jax.numpy as jnp
import numpy as np
from jax import lax
from jax.experimental import pallas as pl
from jax.experimental.pallas import tpu as pltpu
from jax.sharding import PartitionSpec as P

F = 16
KC = 128
SUB = 256
R_DEV = 32
SUB_DEV = 2
SUPPORT = 8
NOVER = 256
CHIP = 2 * R_DEV
LANES = 128
BLOCK = 1024
UNROLL = 8
PART = 512
PART_UNROLL = 16

TWO_PI = 2.0 * math.pi

VMEM = pl.BlockSpec(memory_space=pltpu.VMEM)
HBM = pl.BlockSpec(memory_space=pltpu.HBM)


def turned_rows():
    wave = np.arange(KC)
    place = wave // 8 * 16 + wave % 8
    return np.concatenate([place, place + 8])


def transform_table():
    kcol = np.arange(KC)
    jcol = np.arange(SUB)
    angles = np.float32(TWO_PI) * (kcol[:, None] * jcol[None, :] % SUB).astype(np.float32) / np.float32(SUB)
    scale = np.float32(1.0 / math.sqrt(KC))
    parts = np.concatenate([np.cos(angles) * scale, np.sin(angles) * scale], axis=0).astype(jnp.bfloat16)
    table = np.zeros_like(parts)
    table[turned_rows()] = parts
    return table


EXCHANGES = 4
LATER = 6


def reached(exchange, chip, chips):
    return (
        (chip + 2) % chips,
        (((chip + 1) ^ 1) + chips - 1) % chips,
        (chip + chips - 2) % chips,
        chip ^ 1,
    )[exchange]


def facet_products(factors, rows_ref, outs, half_step, first_row):
    for group in range(R_DEV // 16):
        rows = slice(16 * group, 16 * group + 16)
        cells = jnp.concatenate(
            [rows_ref[0, :, rows, :].reshape(F * 16, KC), rows_ref[1, :, rows, :].reshape(F * 16, KC)], axis=1
        )
        products = []
        for kind in range(2):
            high = jnp.dot(factors(group, 2 * kind), cells, preferred_element_type=jnp.float32)
            low = jnp.dot(factors(group, 2 * kind + 1), cells, preferred_element_type=jnp.float32)
            products.append(high + low)
        with_cos, with_sin = products
        real_part = (with_cos[:, :KC] - with_sin[:, KC:]).astype(jnp.bfloat16)
        imag_part = (with_cos[:, KC:] + with_sin[:, :KC]).astype(jnp.bfloat16)
        for place, out in enumerate(outs):
            for sub in range(SUB_DEV):
                here = slice((place * SUB_DEV + sub) * 16, (place * SUB_DEV + sub) * 16 + 16)
                first = first_row + sub * half_step + 16 * group
                if not isinstance(first, int):
                    first = pl.multiple_of(first, 16)
                out[pl.ds(first, 16), :KC] = real_part[here]
                out[pl.ds(first, 16), KC:] = imag_part[here]


def own_facet_kernel(
    devices,
    start_hbm,
    length_hbm,
    offset_hbm,
    window_hbm,
    rows_hbm,
    *rest,
):
    later_hbm, rest = rest[:LATER], rest[LATER:]
    outs, other_factors, shifts, later = rest[:5], rest[5], rest[6], rest[7 : 7 + LATER]
    start, length, offset, window, rows_ref, own_factors, padded, sems = rest[7 + LATER :]
    copies = [
        pltpu.make_async_copy(source, target, sems.at[number])
        for number, (source, target) in enumerate(
            (
                (start_hbm, start),
                (length_hbm, length),
                (offset_hbm, offset),
                (window_hbm, window),
                (rows_hbm, rows_ref),
                *zip(later_hbm, later),
            )
        )
    ]
    for copy in copies:
        copy.start()
    total_rows = devices * R_DEV
    chips = devices // 2
    position = lax.axis_index("row")
    chip = position // 2
    core = position % 2
    padded[:R_DEV, :] = jnp.zeros((R_DEV, F), jnp.float32)
    padded[R_DEV + SUB :, :] = jnp.zeros((R_DEV, F), jnp.float32)
    row_index = lax.broadcasted_iota(jnp.int32, (R_DEV, F), 0)
    lane = lax.broadcasted_iota(jnp.int32, (R_DEV, LANES), 1)
    sublane = lax.broadcasted_iota(jnp.int32, (R_DEV, LANES), 0)
    diagonal = (lane & 15) == (sublane & 15)

    def spread(values):
        wide = jnp.concatenate([values, jnp.zeros((R_DEV, LANES - F), values.dtype)], axis=1)
        return [
            jnp.concatenate(
                [
                    jnp.take_along_axis(
                        wide[row : row + 8], (lane[:8] >> 4) + 8 * side, axis=1, mode="promise_in_bounds"
                    )
                    for row in range(0, R_DEV, 8)
                ],
                axis=0,
            )
            for side in range(2)
        ]

    for copy in copies[:4]:
        copy.wait()
    padded[R_DEV : R_DEV + SUB, :] = jnp.transpose(window[...])
    for sub in range(SUB_DEV):
        shift = start[position * SUB_DEV + sub] - chip * CHIP
        shifts[sub] = jnp.full((8, LANES), shift, jnp.int32)
    for held, factors in enumerate((own_factors, other_factors)):
        half = core if held == 0 else 1 - core
        base = chip * CHIP + half * R_DEV
        turns = (offset[...] * (base + row_index)) & (total_rows - 1)
        angles = TWO_PI * turns.astype(jnp.float32) / total_rows
        phases = [
            [jnp.where(diagonal, side, 0.0) for side in spread(part)]
            for part in (jnp.cos(angles), jnp.sin(angles))
        ]
        for place in range(1 + EXCHANGES):
            target = chip if place == 0 else reached(place - 1, chip, chips)
            for sub in range(SUB_DEV):
                subgrid = (target * 2 + (core if place == 0 else 1 - core)) * SUB_DEV + sub
                slot = (base - start[subgrid]) & (total_rows - 1)
                slot = jnp.where(slot > total_rows - R_DEV, slot - total_rows, slot)
                slot = jnp.minimum(slot, SUB)
                piece = padded[pl.ds(slot + R_DEV, R_DEV), :]
                weights = spread(jnp.where(slot + row_index < length[subgrid], piece, 0.0))
                for kind in range(2):
                    for side in range(2):
                        exact = weights[side] * phases[kind][side]
                        high = exact.astype(jnp.bfloat16)
                        low = (exact - high.astype(jnp.float32)).astype(jnp.bfloat16)
                        lanes = slice(side * LANES, (side + 1) * LANES)
                        for group in range(R_DEV // 16):
                            rows = slice(16 * group, 16 * group + 16)
                            here = slice((place * SUB_DEV + sub) * 16, (place * SUB_DEV + sub) * 16 + 16)
                            factors[group, 2 * kind, here, lanes] = high[rows]
                            factors[group, 2 * kind + 1, here, lanes] = low[rows]
        if held == 0:
            copies[4].wait()
            facet_products(lambda group, kind: own_factors[group, kind], rows_ref, outs, R_DEV, 0)
    for copy in copies[5:]:
        copy.wait()


def other_facet_kernel(rows_ref, factors, shifts, *rest):
    earlier, outs, shifts_out = rest[:5], rest[5:10], rest[10]
    shifts_out[...] = shifts[...]
    core = lax.axis_index("row") % 2
    for piece, out in zip(earlier, outs):
        for sub in range(SUB_DEV):
            first = pl.multiple_of(sub * CHIP + core * R_DEV, R_DEV)
            out[pl.ds(first, R_DEV), :] = piece[sub * R_DEV : (sub + 1) * R_DEV, :]
    facet_products(lambda group, kind: factors[group, kind], rows_ref, outs, CHIP, (1 - core) * R_DEV)


def spread(low, high, cell, table_row):
    count = cell.shape[1]
    cell = jnp.broadcast_to(cell, (SUPPORT, count))
    table_row = jnp.broadcast_to(table_row, (SUPPORT, count))
    place = table_row & (LANES - 1)
    picked = []
    for first in range(0, count, LANES):
        index = place[:, first : first + LANES]
        from_low = jnp.take_along_axis(low, index, axis=1, mode="promise_in_bounds")
        from_high = jnp.take_along_axis(high, index, axis=1, mode="promise_in_bounds")
        picked.append(jnp.where(table_row[:, first : first + LANES] < LANES, from_low, from_high))
    weights = jnp.concatenate(picked, axis=1)
    for bit in range(3):
        turned = pltpu.roll(weights, 1 << bit, axis=0)
        weights = jnp.where((cell & (1 << bit)) != 0, turned, weights)
    sublane = lax.broadcasted_iota(jnp.int32, (SUPPORT, count), 0)
    tile = ((cell >> 3) + jnp.where(sublane < (cell & 7), 1, 0)) & (SUB // 8 - 1)
    odd = (tile & 1) != 0
    pair = (tile >> 1).astype(jnp.float32)
    pairs = jnp.concatenate([jnp.where(odd, -1.0, pair), jnp.where(odd, pair, -1.0)], axis=0).astype(jnp.bfloat16)
    both = jnp.concatenate([weights, weights], axis=0).astype(jnp.bfloat16)
    zero = jnp.zeros_like(both)
    return jnp.concatenate([jnp.where(pairs == jnp.bfloat16(t), both, zero) for t in range(SUB // 16)], axis=0)


def spread_kernel(
    shifts_ref,
    table_ref,
    transform_ref,
    row_ref,
    column_ref,
    row_kernel_ref,
    column_kernel_ref,
    row_spread,
    column_waves,
):
    low, high = table_ref[:, :LANES], table_ref[:, LANES:]

    def one_block(block, carry):
        lanes = pl.ds(pl.multiple_of(block * BLOCK, BLOCK), BLOCK)
        for sub in range(SUB_DEV):
            shift = jnp.concatenate([shifts_ref[sub, :1, :]] * (BLOCK // LANES), axis=1)
            cell_row = (row_ref[sub : sub + 1, lanes] + shift) & (SUB - 1)
            row_spread[sub, :, lanes] = spread(low, high, cell_row, row_kernel_ref[sub : sub + 1, lanes])
            columns = spread(low, high, column_ref[sub : sub + 1, lanes], column_kernel_ref[sub : sub + 1, lanes])
            column_waves[sub, :, lanes] = jnp.dot(transform_ref[...], columns, preferred_element_type=jnp.float32)
        return carry

    lax.fori_loop(0, row_ref.shape[1] // BLOCK, one_block, 0, unroll=UNROLL)


def degrid_kernel(
    per_dest,
    own_ref,
    far_below_ref,
    odd_edge_ref,
    far_above_ref,
    even_edge_ref,
    row_spread,
    column_waves,
    out_ref,
    waves,
    gathered,
):
    even = lax.axis_index("row") // 2 % 2 == 0
    wave = lax.broadcasted_iota(jnp.int32, (2 * KC, 2 * KC), 1)
    place = ((wave & (KC - 1)) >> 3) * 16 + (wave & 7) + jnp.where(wave < KC, 0, 8)
    turn = (lax.broadcasted_iota(jnp.int32, (2 * KC, 2 * KC), 0) == place).astype(jnp.float32).astype(jnp.bfloat16)
    for sub in range(SUB_DEV):
        rows = slice(sub * CHIP, sub * CHIP + CHIP)
        odd_edge, even_edge = odd_edge_ref[rows, :], even_edge_ref[rows, :]
        summed = jnp.concatenate(
            [
                own_ref[rows, :],
                jnp.where(even, even_edge, odd_edge),
                far_below_ref[rows, :] + far_above_ref[rows, :],
                jnp.where(even, odd_edge, even_edge),
            ],
            axis=0,
        )
        waves[sub] = lax.dot_general(
            turn, summed, (((1,), (1,)), ((), ())), preferred_element_type=jnp.float32
        ).astype(jnp.bfloat16)
    chunks = per_dest // LANES

    def one_block(block, carry):
        lanes = pl.ds(pl.multiple_of(block * PART, PART), PART)
        for sub in range(SUB_DEV):
            along = jnp.dot(waves[sub], row_spread[sub, :, lanes], preferred_element_type=jnp.float32)
            halves = [[None, None], [None, None]]
            for t in range(KC // 8):
                real = slice(16 * t, 16 * t + 8)
                imag = slice(16 * t + 8, 16 * t + 16)
                real_wave = column_waves[sub, real, lanes]
                imag_wave = column_waves[sub, imag, lanes]
                terms = (
                    along[real] * real_wave - along[imag] * imag_wave,
                    along[real] * imag_wave + along[imag] * real_wave,
                )
                halves[t % 2] = [term if t < 2 else total + term for total, term in zip(halves[t % 2], terms)]
            sums = [first_half + second_half for first_half, second_half in zip(*halves)]
            first = block * (PART // LANES * 4)
            for part in range(2):
                total = jnp.sum(sums[part], axis=0, keepdims=True)
                for place in range(PART // LANES):
                    row = place // chunks * 4 * chunks + (sub * 2 + part) * chunks + place % chunks
                    gathered[pl.ds(first + row, 1), :] = total[:, place * LANES : (place + 1) * LANES]
        return carry

    lax.fori_loop(0, row_spread.shape[2] // PART, one_block, 0, unroll=PART_UNROLL)
    out_ref[...] = gathered[...].astype(jnp.bfloat16)


def place_kernel(devices, chunks, in_ref, out_ref, wide):
    wide[...] = in_ref[...].astype(jnp.float32)
    for part in range(2):
        for chunk in range(chunks):
            out_ref[part, :, chunk * LANES : (chunk + 1) * LANES] = wide[
                pl.ds(part * chunks + chunk, devices * SUB_DEV, stride=2 * chunks), :
            ]


def local(
    facet_rows,
    range_start,
    range_length,
    facet_offset,
    window_table,
    kernel_table,
    cell_row,
    cell_column,
    kernel_row,
    kernel_column,
):
    devices = lax.axis_size("row")
    chips = devices // 2
    slots = cell_row.shape[1]
    per_dest = slots // devices
    chunks = per_dest // LANES
    other_rows = lax.ppermute(facet_rows, "row", [(i, i ^ 1) for i in range(devices)])
    small = pltpu.CompilerParams(vmem_limit_bytes=12 * 1024 * 1024)
    factors = jax.ShapeDtypeStruct((R_DEV // 16, 4, 5 * SUB_DEV * 16, 16 * F), jnp.bfloat16)
    later = (kernel_table.T, jnp.asarray(transform_table()), cell_row, cell_column, kernel_row, kernel_column)
    *own_pieces, other_factors, shifts, table, transform, rows, columns, row_kernels, column_kernels = pl.pallas_call(
        lambda *refs: own_facet_kernel(devices, *refs),
        out_shape=[jax.ShapeDtypeStruct((SUB_DEV * R_DEV, 2 * KC), jnp.bfloat16)] * 5
        + [factors, jax.ShapeDtypeStruct((SUB_DEV, 8, LANES), jnp.int32)]
        + [jax.ShapeDtypeStruct(value.shape, value.dtype) for value in later],
        in_specs=[HBM] * (5 + LATER),
        out_specs=[VMEM] * (7 + LATER),
        scratch_shapes=[
            pltpu.SMEM(range_start.shape, jnp.int32),
            pltpu.SMEM(range_length.shape, jnp.int32),
            pltpu.VMEM((1, F), jnp.int32),
            pltpu.VMEM(window_table.shape, jnp.float32),
            pltpu.VMEM(facet_rows.shape, jnp.bfloat16),
            pltpu.VMEM(factors.shape, jnp.bfloat16),
            pltpu.VMEM((SUB + 2 * R_DEV, F), jnp.float32),
            pltpu.SemaphoreType.DMA((5 + LATER,)),
        ],
        compiler_params=small,
        name="own_facet_sums",
    )(
        *(
            pltpu.with_memory_space_constraint(value, pltpu.HBM)
            for value in (range_start, range_length, facet_offset.reshape(1, F), window_table, facet_rows, *later)
        )
    )
    *pieces, shifts = pl.pallas_call(
        other_facet_kernel,
        out_shape=[jax.ShapeDtypeStruct((SUB_DEV * CHIP, 2 * KC), jnp.bfloat16)] * 5
        + [jax.ShapeDtypeStruct((SUB_DEV, 8, LANES), jnp.int32)],
        in_specs=[VMEM] * 8,
        out_specs=[VMEM] * 6,
        compiler_params=small,
        name="other_facet_sums",
    )(other_rows, other_factors, shifts, *own_pieces)
    came = []
    for exchange, piece in enumerate(pieces[1:]):
        pairs = [
            (2 * chip + core, 2 * reached(exchange, chip, chips) + 1 - core)
            for chip in range(chips)
            for core in range(2)
        ]
        came.append(lax.ppermute(piece, "row", pairs))
    rows_out = devices * 4 * chunks
    spread_shape = (SUB_DEV, SUB, slots)
    row_spread, column_waves = pl.pallas_call(
        spread_kernel,
        out_shape=[
            jax.ShapeDtypeStruct(spread_shape, jnp.bfloat16),
            jax.ShapeDtypeStruct(spread_shape, jnp.float32),
        ],
        in_specs=[VMEM] * 7,
        out_specs=[VMEM] * 2,
        compiler_params=small,
        cost_estimate=pl.CostEstimate(
            flops=2 * SUB_DEV * SUB * 2 * KC * slots, bytes_accessed=6 * SUB_DEV * SUB * slots, transcendentals=0
        ),
        name="spread",
    )(shifts, table, transform, rows, columns, row_kernels, column_kernels)
    results = pl.pallas_call(
        lambda *refs: degrid_kernel(per_dest, *refs),
        out_shape=jax.ShapeDtypeStruct((rows_out, LANES), jnp.bfloat16),
        in_specs=[VMEM] * 7,
        out_specs=VMEM,
        scratch_shapes=[
            pltpu.VMEM((SUB_DEV, 2 * KC, SUB), jnp.bfloat16),
            pltpu.VMEM((rows_out, LANES), jnp.float32),
        ],
        compiler_params=small,
        name="degrid",
    )(pieces[0], *came, row_spread, column_waves)
    received = lax.all_to_all(
        results.reshape(devices, 4 * chunks, LANES), "row", split_axis=0, concat_axis=0, tiled=True
    )
    return pl.pallas_call(
        lambda *refs: place_kernel(devices, chunks, *refs),
        out_shape=jax.ShapeDtypeStruct((2, devices * SUB_DEV, per_dest), jnp.float32),
        in_specs=[VMEM],
        out_specs=VMEM,
        scratch_shapes=[pltpu.VMEM((rows_out, LANES), jnp.float32)],
        compiler_params=small,
        name="place",
    )(received.reshape(rows_out, LANES))


def solution(mesh):
    placed = (
        P(None, None, ("grp", "row"), None),
        P("grp"),
        P("grp"),
        P("grp"),
        P(),
        P(),
        P(("grp", "row"), None),
        P(("grp", "row"), None),
        P(("grp", "row"), None),
        P(("grp", "row"), None),
    )
    return jax.shard_map(
        local, mesh=mesh, in_specs=placed, out_specs=P(None, "grp", "row"), check_vma=False
    )
```
